128 devices in a mesh: rows: 32 (over z, x, core), vec: 4 (over y).
Axes of the slice: x: 4, y: 4, z: 4, core: 2. Of those that a mesh axis runs over, the one named last changes fastest.
Arguments:
- lattice_state: float32 [2, 512, 4096], P(None, 'rows'), may hold values from -0.6 to 0.6
- constant_field: float32 [2, 512, 4096], P(None, 'rows'), may hold values from -0.4 to 0.4
- tangents: float32 [32, 2, 512, 4096], P('vec', None, 'rows'), may hold values from -6 to 6
Outputs:
- next_state: float32 [2, 512, 4096], P(None, 'rows')
- basis: float32 [32, 2, 512, 4096], P('vec', None, 'rows')
- growth: float32 [32], replicated
The draws below stay inside these ranges and needn't reach their ends.
All inputs are finite; a program needn't handle non-finite values.
Results may differ from the reference program's by a relative error of at most 0.00028.
Values sent between devices are 32-bit elements; how exact they have to be, the bound alone decides.
No kernel may reach another device: no remote copies, remote signals or barrier semaphores. Data moves between devices by JAX's collectives and lax.ppermute only.
A program may use at most 128 MiB of HBM per device.

```python
import math
import jax
import jax.numpy as jnp
from jax import lax

NC = 4096
NV = 32
STEPS = 3
NR = 512


def levels(key, extent, pieces, smallest, high):
    gain, own = 1.0, jax.random.fold_in(key, 6)
    for position, shards_of in pieces:
        heights = jnp.exp(jax.random.uniform(jax.random.fold_in(own, position), (shards_of,), jnp.float32, smallest / len(pieces), high / len(pieces)))
        gain = gain * jnp.repeat(heights, extent[position] // shards_of).reshape([-1 if axis == position else 1 for axis in range(len(extent))])
    return gain


def gaussian(rng, shape, spread, bound, cuts=(), kind=jnp.bfloat16):
    gain = levels(rng, shape, cuts, -0.22, 0.18) if cuts else 1.0
    entries = jax.random.normal(rng, shape, jnp.float32) * spread * gain
    return jnp.minimum(jnp.maximum(entries, -bound), bound).astype(kind)


def setup_inputs(seed: int = 0) -> dict:
    key_list = jax.random.split(jax.random.key(seed), 4)
    return {
        "lattice_state": jnp.clip(jax.random.uniform(key_list[0], (2, NR, NC), jnp.float32, -0.6, 0.6) * levels(key_list[0], (2, NR, NC), ((1, 32),), -0.4, 0.0), -0.6, 0.6),
        "constant_field": jnp.clip(jax.random.uniform(key_list[1], (2, NR, NC), jnp.float32, -0.4, 0.4) * levels(key_list[1], (2, NR, NC), ((1, 32),), -0.4, 0.0), -0.4, 0.4),
        "tangents": gaussian(key_list[2], (NV, 2, NR, NC), 1.0, 6.0, ((0, 4), (2, 32)), jnp.float32),
    }


COUPLING = 0.35

def mix_full(field):
    beside = jnp.roll(field, 1, -2) + jnp.roll(field, -1, -2) + jnp.roll(field, 1, -1) + jnp.roll(field, -1, -1)
    return (1.0 - COUPLING) * field + COUPLING / 4.0 * beside

def reference(lattice_state, constant_field, tangents):
    current = lattice_state
    driven = tangents
    for lattice_step in range(STEPS):
        real_z = current[0]
        imag_z = current[1]
        map_real = real_z * real_z - imag_z * imag_z + constant_field[0]
        map_imag = 2.0 * real_z * imag_z + constant_field[1]
        real_u = driven[:, 0]
        imag_u = driven[:, 1]
        push_real = 2.0 * (real_z * real_u - imag_z * imag_u)
        push_imag = 2.0 * (real_z * imag_u + imag_z * real_u)
        current = mix_full(jnp.stack([map_real, map_imag]))
        driven = mix_full(jnp.stack([push_real, push_imag], axis=1))
    gram_matrix = jnp.einsum('jabc,kabc->jk', driven, driven, precision=lax.Precision.HIGHEST)
    factor = jnp.linalg.cholesky(gram_matrix)
    identity = jnp.eye(NV, dtype=jnp.float32)
    inverse = jax.scipy.linalg.solve_triangular(factor, identity, lower=True).T
    norm_scale = math.sqrt(2.0 * NR * NC)
    basis = norm_scale * jnp.einsum('jk,jabc->kabc', inverse, driven, precision=lax.Precision.HIGHEST)
    growth = jnp.log(jnp.diagonal(factor) / norm_scale)
    return (current, basis, growth)
```

```python
import math

import jax
import jax.numpy as jnp
from jax import lax
from jax.experimental import pallas as pl
from jax.experimental.pallas import tpu as pltpu
from jax.sharding import PartitionSpec as P

NV = 32
STEPS = 3
COUPLING = 0.35
HALO = 4
VMEM = 56 * 1024 * 1024
HIGHEST = lax.Precision.HIGHEST
FULL = pl.BlockSpec(memory_space=pltpu.VMEM)
SMEM = pl.BlockSpec(memory_space=pltpu.SMEM)


def params():
    return pltpu.CompilerParams(vmem_limit_bytes=VMEM)


def neighbours(block):
    count = lax.axis_size("rows")
    forward = [(i, (i + 1) % count) for i in range(count)]
    backward = [(target, source) for source, target in forward]
    last = lax.slice_in_dim(block, block.shape[2] - HALO, None, axis=2)
    first = lax.slice_in_dim(block, 0, HALO, axis=2)
    above = lax.ppermute(last, "rows", forward)
    below = lax.ppermute(first, "rows", backward)
    return below, above


def mix(field):
    rows, columns = field.shape
    beside = (
        pltpu.roll(field, 1, 0)
        + pltpu.roll(field, rows - 1, 0)
        + pltpu.roll(field, 1, 1)
        + pltpu.roll(field, columns - 1, 1)
    )
    return (1.0 - COUPLING) * field + (COUPLING / 4.0) * beside


def ring(block, below, above):
    return jnp.concatenate([block, below, above], axis=0)


def lattice_kernel(z_ref, c_ref, below_ref, above_ref, twice_ref, next_ref):
    real, imag = (ring(z_ref[i], below_ref[0, i], above_ref[0, i]) for i in range(2))
    const_real, const_imag = (ring(c_ref[i], below_ref[1, i], above_ref[1, i]) for i in range(2))
    for step in range(STEPS):
        twice_ref[step, 0] = 2.0 * real
        twice_ref[step, 1] = 2.0 * imag
        map_real = real * real - imag * imag + const_real
        map_imag = 2.0 * real * imag + const_imag
        real, imag = mix(map_real), mix(map_imag)
    rows = z_ref.shape[1]
    next_ref[0] = real[:rows]
    next_ref[1] = imag[:rows]


def tangent_kernel(me_ref, u_ref, below_ref, above_ref, twice_ref, *rest):
    outs, slabs = rest[:-1], rest[-1]
    real, imag = (ring(u_ref[0, i], below_ref[0, i], above_ref[0, i]) for i in range(2))
    for step in range(STEPS):
        z_real, z_imag = twice_ref[step, 0], twice_ref[step, 1]
        push_real = z_real * real - z_imag * imag
        push_imag = z_real * imag + z_imag * real
        real, imag = mix(push_real), mix(push_imag)
    slabs[0] = real[:8]
    slabs[1] = real[8:16]
    slabs[2] = imag[:8]
    slabs[3] = imag[8:16]
    for shift, out in enumerate(outs):
        out[0] = slabs[lax.rem(me_ref[0] + shift, 4)]


def push(me, vectors, halo, twice, start, count):
    columns = vectors.shape[-1]
    return pl.pallas_call(
        tangent_kernel,
        grid=(count,),
        in_specs=[
            SMEM,
            pl.BlockSpec((1, 2, 16, columns), lambda i: (start + i, 0, 0, 0)),
            pl.BlockSpec((1, 2, HALO, columns), lambda i: (i, 0, 0, 0)),
            pl.BlockSpec((1, 2, HALO, columns), lambda i: (i, 0, 0, 0)),
            FULL,
        ],
        out_specs=[pl.BlockSpec((1, 8, columns), lambda i: (i, 0, 0))] * 4,
        out_shape=[jax.ShapeDtypeStruct((count, 8, columns), jnp.float32)] * 4,
        scratch_shapes=[pltpu.VMEM((4, 8, columns), jnp.float32)],
        compiler_params=params(),
        cost_estimate=pl.CostEstimate(
            flops=count * 2_000_000, bytes_accessed=count * 2_000_000, transcendentals=0
        ),
    )(me, vectors, *halo, twice)


def same_row(shape, period):
    return lax.rem(lax.broadcasted_iota(jnp.int32, shape, 0), period) == lax.rem(
        lax.broadcasted_iota(jnp.int32, shape, 1), period
    )


def owner(shape, group):
    row = lax.broadcasted_iota(jnp.int32, shape, 0)
    column = lax.broadcasted_iota(jnp.int32, shape, 1)
    return jnp.where(row == lax.div(column, group), 1.0, 0.0)


def gram_kernel(chunks, me_ref, *refs):
    pieces = refs[: 4 * chunks]
    high_ref, low_ref, gram_ref = refs[4 * chunks :]
    for chunk in range(chunks):
        for shift in range(4):
            piece = pieces[4 * chunk + shift]
            count, rows, columns = piece.shape
            source = lax.rem(me_ref[0] + 4 - shift, 4)
            start = pl.multiple_of(source * 64 + chunk * count * rows, count * rows)
            value = piece[...].reshape(count * rows, columns)
            high = value.astype(jnp.bfloat16)
            low = (value - high.astype(jnp.float32)).astype(jnp.bfloat16)
            high_ref[pl.ds(start, count * rows), :] = high
            low_ref[pl.ds(start, count * rows), :] = low
    high = high_ref[...]
    low = low_ref[...]
    last = (((1,), (1,)), ((), ()))
    main = lax.dot_general(high, high, last, preferred_element_type=jnp.float32)
    rest = lax.dot_general(high, low, last, preferred_element_type=jnp.float32)
    full = main + (rest + rest.T)
    full = jnp.where(same_row(full.shape, 8), full, 0.0)
    left = full.reshape(NV, 8, 8 * NV).sum(1)
    gram_ref[...] = lax.dot_general(
        left, owner((NV, 8 * NV), 8), last, precision=HIGHEST, preferred_element_type=jnp.float32
    )


def inner_products(me, pieces, chunks):
    columns = pieces[0].shape[-1]
    return pl.pallas_call(
        lambda *refs: gram_kernel(chunks, *refs),
        in_specs=[SMEM] + [FULL] * len(pieces),
        out_specs=[FULL] * 3,
        out_shape=[
            jax.ShapeDtypeStruct((8 * NV, columns), jnp.bfloat16),
            jax.ShapeDtypeStruct((8 * NV, columns), jnp.bfloat16),
            jax.ShapeDtypeStruct((NV, NV), jnp.float32),
        ],
        compiler_params=params(),
    )(me, *pieces)


def basis_kernel(scale, me_ref, gram_ref, high_ref, low_ref, growth_ref, *rest):
    outs, w_high, w_low = rest[:-2], rest[-2], rest[-1]
    row = lax.broadcasted_iota(jnp.int32, (NV, 2 * NV), 0)
    column = lax.broadcasted_iota(jnp.int32, (NV, 2 * NV), 1)
    identity = jnp.where(column == row + NV, 1.0, 0.0)
    spread = jnp.where(
        lax.broadcasted_iota(jnp.int32, (NV, 2 * NV), 0)
        == lax.broadcasted_iota(jnp.int32, (NV, 2 * NV), 1),
        1.0,
        0.0,
    )
    last = (((1,), (0,)), ((), ()))
    work = identity + lax.dot_general(
        gram_ref[...], spread, last, precision=HIGHEST, preferred_element_type=jnp.float32
    )
    for k in range(NV):
        pivot_row = work[k : k + 1, :]
        pivot = pivot_row[:, k : k + 1]
        inverse = lax.rsqrt(pivot)
        inverse = inverse * (1.5 - 0.5 * pivot * inverse * inverse)
        scaled = pivot_row * inverse
        factor = work[:, k : k + 1] * inverse
        work = jnp.where(row > k, work - factor * scaled, jnp.where(row == k, scaled, work))
    diagonal = jnp.sum(jnp.where(column == row, work, 0.0), axis=0, keepdims=True)
    growth_ref[...] = jnp.log(diagonal[:, :NV] / scale)
    inverse = work[:, NV:] * scale
    group = owner((NV, 8 * NV), 8)
    wide = lax.dot_general(
        inverse, group, last, precision=HIGHEST, preferred_element_type=jnp.float32
    )
    tall = jnp.broadcast_to(wide[:, None, :], (NV, 8, 8 * NV)).reshape(8 * NV, 8 * NV)
    weights = jnp.where(same_row(tall.shape, 8), tall, 0.0)
    high = weights.astype(jnp.bfloat16)
    w_high[...] = high
    w_low[...] = (weights - high.astype(jnp.float32)).astype(jnp.bfloat16)
    for shift, out in enumerate(outs):
        start = pl.multiple_of(lax.rem(me_ref[0] + shift, 4) * 64, 64)
        own_high = w_high[pl.ds(start, 64), :]
        own_low = w_low[pl.ds(start, 64), :]
        value = jnp.dot(own_high, high_ref[...], preferred_element_type=jnp.float32)
        value += jnp.dot(own_high, low_ref[...], preferred_element_type=jnp.float32)
        value += jnp.dot(own_low, high_ref[...], preferred_element_type=jnp.float32)
        out[...] = value.reshape(out.shape)


def orthonormal(me, gram, high, low, scale):
    columns = high.shape[-1]
    return pl.pallas_call(
        lambda *refs: basis_kernel(scale, *refs),
        in_specs=[SMEM] + [FULL] * 3,
        out_specs=[FULL] * 5,
        out_shape=[jax.ShapeDtypeStruct((1, NV), jnp.float32)]
        + [jax.ShapeDtypeStruct((8, 8, columns), jnp.float32)] * 4,
        scratch_shapes=[pltpu.VMEM((8 * NV, 8 * NV), jnp.bfloat16)] * 2,
        compiler_params=params(),
    )(me, gram, high, low)


def assemble_kernel(me_ref, *refs):
    pieces, out = refs[:-1], refs[-1]
    for shift, piece in enumerate(pieces):
        slab = lax.rem(me_ref[0] + 4 - shift, 4)
        out[:, slab] = piece[...]


def assemble(me, pieces):
    count, rows, columns = pieces[0].shape
    step = 2
    return pl.pallas_call(
        assemble_kernel,
        grid=(count // step,),
        in_specs=[SMEM] + [pl.BlockSpec((step, rows, columns), lambda i: (i, 0, 0))] * 4,
        out_specs=pl.BlockSpec((step, 4, rows, columns), lambda i: (i, 0, 0, 0)),
        out_shape=jax.ShapeDtypeStruct((count, 4, rows, columns), jnp.float32),
        compiler_params=params(),
    )(me, *pieces)


def shifted(block, shift):
    return lax.ppermute(block, "vec", [(i, (i + shift) % 4) for i in range(4)])


def exchange(blocks):
    moved = {shift: shifted(blocks[shift], shift) for shift in (2, 1, 3)}
    return [blocks[0], moved[1], moved[2], moved[3]]


def group_sum(value, axis, stride, members):
    size = lax.axis_size(axis)
    terms = [value] + [
        lax.ppermute(value, axis, [(i, i ^ (k * stride)) for i in range(size)])
        for k in range(1, members)
    ]
    while len(terms) > 1:
        terms = [terms[i] + terms[i + 1] for i in range(0, len(terms), 2)]
    return terms[0]


def total_sum(value):
    value = group_sum(value, "vec", 1, 4)
    value = group_sum(value, "rows", 1, 2)
    value = group_sum(value, "rows", 2, 4)
    return group_sum(value, "rows", 8, 4)


CHUNKS = (4, 4)


def per_device(lattice_state, constant_field, tangents):
    me = lax.axis_index("vec").astype(jnp.int32).reshape(1)
    rows, columns = lattice_state.shape[1:]
    scale = math.sqrt(2.0 * rows * lax.axis_size("rows") * columns)
    fields = jnp.stack([lattice_state, constant_field])
    below, above = neighbours(fields)
    halos, start = [], 0
    for count in CHUNKS:
        halos.append(neighbours(lax.slice_in_dim(tangents, start, start + count, axis=0)))
        start += count
    twice, next_state = pl.pallas_call(
        lattice_kernel,
        in_specs=[FULL] * 4,
        out_specs=[FULL] * 2,
        out_shape=[
            jax.ShapeDtypeStruct((STEPS, 2, rows + 2 * HALO, columns), jnp.float32),
            jax.ShapeDtypeStruct((2, rows, columns), jnp.float32),
        ],
        compiler_params=params(),
    )(lattice_state, constant_field, below, above)
    pieces, start = [], 0
    for count, halo in zip(CHUNKS, halos):
        pieces += exchange(push(me, tangents, halo, twice, start, count))
        start += count
    high, low, partial_gram = inner_products(me, pieces, len(CHUNKS))
    gram = total_sum(partial_gram)
    growth, *parts = orthonormal(me, gram, high, low, scale)
    basis = assemble(me, exchange(parts))
    return (next_state, basis.reshape(tangents.shape), growth.reshape(NV))


def solution(mesh):
    return jax.shard_map(
        per_device,
        mesh=mesh,
        in_specs=(P(None, "rows", None), P(None, "rows", None), P("vec", None, "rows", None)),
        out_specs=(P(None, "rows", None), P("vec", None, "rows", None), P()),
        check_vma=False,
    )
```

```python
import math

import jax
import jax.numpy as jnp
from jax import lax
from jax.experimental import pallas as pl
from jax.experimental.pallas import tpu as pltpu
from jax.sharding import PartitionSpec as P

NV = 32
STEPS = 3
COUPLING = 0.35
HALO = 4
VMEM = 24 * 1024 * 1024
HIGHEST = lax.Precision.HIGHEST
FULL = pl.BlockSpec(memory_space=pltpu.VMEM)
SMEM = pl.BlockSpec(memory_space=pltpu.SMEM)


def params():
    return pltpu.CompilerParams(vmem_limit_bytes=VMEM)


def edges(block):
    last = lax.slice_in_dim(block, block.shape[2] - HALO, None, axis=2)
    return last, lax.slice_in_dim(block, 0, HALO, axis=2)


def neighbours(last, first):
    count = lax.axis_size("rows")
    forward = [(i, (i + 1) % count) for i in range(count)]
    backward = [(target, source) for source, target in forward]
    above = lax.ppermute(last, "rows", forward)
    below = lax.ppermute(first, "rows", backward)
    return below, above


def mix(field):
    rows, columns = field.shape
    beside = (
        pltpu.roll(field, 1, 0)
        + pltpu.roll(field, rows - 1, 0)
        + pltpu.roll(field, 1, 1)
        + pltpu.roll(field, columns - 1, 1)
    )
    return (1.0 - COUPLING) * field + (COUPLING / 4.0) * beside


def ring(block, below, above):
    return jnp.concatenate([block, below, above], axis=0)


def lattice_kernel(z_ref, c_ref, below_ref, above_ref, twice_ref, next_ref):
    real, imag = (ring(z_ref[i], below_ref[0, i], above_ref[0, i]) for i in range(2))
    const_real, const_imag = (ring(c_ref[i], below_ref[1, i], above_ref[1, i]) for i in range(2))
    for step in range(STEPS):
        twice_ref[step, 0] = 2.0 * real
        twice_ref[step, 1] = 2.0 * imag
        map_real = real * real - imag * imag + const_real
        map_imag = 2.0 * real * imag + const_imag
        real, imag = mix(map_real), mix(map_imag)
    rows = z_ref.shape[1]
    next_ref[0] = real[:rows]
    next_ref[1] = imag[:rows]


def tangent_kernel(me_ref, u_ref, below_ref, above_ref, twice_ref, *rest):
    outs, slabs = rest[:-1], rest[-1]
    real, imag = (ring(u_ref[0, i], below_ref[0, i], above_ref[0, i]) for i in range(2))
    for step in range(STEPS):
        z_real, z_imag = twice_ref[step, 0], twice_ref[step, 1]
        push_real = z_real * real - z_imag * imag
        push_imag = z_real * imag + z_imag * real
        real, imag = mix(push_real), mix(push_imag)
    slabs[0] = real[:8]
    slabs[1] = real[8:16]
    slabs[2] = imag[:8]
    slabs[3] = imag[8:16]
    for shift, out in enumerate(outs):
        out[0] = slabs[lax.rem(me_ref[0] + shift, 4)]


def push(me, vectors, halo, twice, start, count):
    columns = vectors.shape[-1]
    skip = halo[0].shape[0] - count
    return pl.pallas_call(
        tangent_kernel,
        grid=(count,),
        in_specs=[
            SMEM,
            pl.BlockSpec((1, 2, 16, columns), lambda i: (start + i, 0, 0, 0)),
            pl.BlockSpec((1, 2, HALO, columns), lambda i: (skip + i, 0, 0, 0)),
            pl.BlockSpec((1, 2, HALO, columns), lambda i: (skip + i, 0, 0, 0)),
            FULL,
        ],
        out_specs=[pl.BlockSpec((1, 8, columns), lambda i: (i, 0, 0))] * 4,
        out_shape=[jax.ShapeDtypeStruct((count, 8, columns), jnp.float32)] * 4,
        scratch_shapes=[pltpu.VMEM((4, 8, columns), jnp.float32)],
        compiler_params=params(),
        cost_estimate=pl.CostEstimate(
            flops=count * 30_000_000, bytes_accessed=count * 6_000_000, transcendentals=0
        ),
    )(me, pltpu.with_memory_space_constraint(vectors, pltpu.HBM), *halo, twice)


def same_row(shape, period):
    return lax.rem(lax.broadcasted_iota(jnp.int32, shape, 0), period) == lax.rem(
        lax.broadcasted_iota(jnp.int32, shape, 1), period
    )


def owner(shape, group):
    row = lax.broadcasted_iota(jnp.int32, shape, 0)
    column = lax.broadcasted_iota(jnp.int32, shape, 1)
    return jnp.where(row == lax.div(column, group), 1.0, 0.0)


def split(value):
    high = value.astype(jnp.bfloat16)
    return high, (value - high.astype(jnp.float32)).astype(jnp.bfloat16)


def gram_kernel(chunks, me_ref, *refs):
    pieces = refs[: 4 * chunks]
    high_ref, low_ref, gram_ref = refs[4 * chunks :]
    offset = 0
    for chunk in range(chunks):
        count, rows, columns = pieces[4 * chunk].shape
        for shift in range(4):
            source = lax.rem(me_ref[0] + 4 - shift, 4)
            start = pl.multiple_of(source * 64 + offset, 16)
            high, low = split(pieces[4 * chunk + shift][...].reshape(count * rows, columns))
            high_ref[pl.ds(start, count * rows), :] = high
            low_ref[pl.ds(start, count * rows), :] = low
        offset += count * rows
    high = high_ref[...]
    low = low_ref[...]
    last = (((1,), (1,)), ((), ()))
    main = lax.dot_general(high, high, last, preferred_element_type=jnp.float32)
    rest = lax.dot_general(high, low, last, preferred_element_type=jnp.float32)
    full = main + (rest + rest.T)
    full = jnp.where(same_row(full.shape, 8), full, 0.0)
    left = full.reshape(NV, 8, 8 * NV).sum(1)
    gram = lax.dot_general(
        left, owner((NV, 8 * NV), 8), last, precision=HIGHEST, preferred_element_type=jnp.float32
    )
    packed = jnp.concatenate([gram[8 * i : 8 * i + 8] for i in range(4)], axis=1)
    copies = gram_ref.shape[0] // 8
    gram_ref[...] = jnp.broadcast_to(packed[None], (copies, 8, 4 * NV)).reshape(gram_ref.shape)


def inner_products(me, pieces, chunks):
    columns = pieces[0].shape[-1]
    devices = lax.axis_size("rows") * lax.axis_size("vec")
    return pl.pallas_call(
        lambda *refs: gram_kernel(chunks, *refs),
        in_specs=[SMEM] + [FULL] * len(pieces),
        out_specs=[FULL] * 3,
        out_shape=[
            jax.ShapeDtypeStruct((8 * NV, columns), jnp.bfloat16),
            jax.ShapeDtypeStruct((8 * NV, columns), jnp.bfloat16),
            jax.ShapeDtypeStruct((8 * devices, 4 * NV), jnp.float32),
        ],
        compiler_params=params(),
    )(me, *pieces)


def factor_kernel(scale, terms_ref, growth_ref, high_ref, low_ref):
    row = lax.broadcasted_iota(jnp.int32, (NV, 2 * NV), 0)
    column = lax.broadcasted_iota(jnp.int32, (NV, 2 * NV), 1)
    spread = jnp.where(row == column, 1.0, 0.0)
    last = (((1,), (0,)), ((), ()))
    packed = jnp.sum(terms_ref[...].reshape(terms_ref.shape[0] // 8, 8, 4 * NV), axis=0)
    gram = jnp.concatenate([packed[:, NV * i : NV * i + NV] for i in range(4)], axis=0)
    work = jnp.where(column == row + NV, 1.0, 0.0) + lax.dot_general(
        gram, spread, last, precision=HIGHEST, preferred_element_type=jnp.float32
    )
    for k in range(NV):
        pivot_row = work[k : k + 1, :]
        pivot = pivot_row[:, k : k + 1]
        inverse = lax.rsqrt(pivot)
        inverse = inverse * (1.5 - 0.5 * pivot * inverse * inverse)
        scaled = pivot_row * inverse
        factor = work[:, k : k + 1] * inverse
        work = jnp.where(row > k, work - factor * scaled, jnp.where(row == k, scaled, work))
    diagonal = jnp.sum(jnp.where(column == row, work, 0.0), axis=0, keepdims=True)
    growth_ref[...] = jnp.log(diagonal[:, :NV] / scale)
    inverse = work[:, NV:] * scale
    wide = lax.dot_general(
        inverse,
        owner((NV, 8 * NV), 8),
        last,
        precision=HIGHEST,
        preferred_element_type=jnp.float32,
    )
    tall = jnp.broadcast_to(wide[:, None, :], (NV, 8, 8 * NV)).reshape(8 * NV, 8 * NV)
    weights = jnp.where(same_row(tall.shape, 8), tall, 0.0)
    high = weights.astype(jnp.bfloat16)
    high_ref[...] = high
    low_ref[...] = (weights - high.astype(jnp.float32)).astype(jnp.bfloat16)


def factorise(terms, scale):
    return pl.pallas_call(
        lambda *refs: factor_kernel(scale, *refs),
        in_specs=[FULL],
        out_specs=[FULL] * 3,
        out_shape=[jax.ShapeDtypeStruct((1, NV), jnp.float32)]
        + [jax.ShapeDtypeStruct((8 * NV, 8 * NV), jnp.bfloat16)] * 2,
        compiler_params=params(),
    )(terms)


def product(w_high, w_low, high, low):
    value = jnp.dot(w_high, high, preferred_element_type=jnp.float32)
    value += jnp.dot(w_high, low, preferred_element_type=jnp.float32)
    return value + jnp.dot(w_low, high, preferred_element_type=jnp.float32)


def send_kernel(me_ref, w_high, w_low, high_ref, low_ref, next_ref, across_ref, previous_ref):
    for shift, out in ((1, next_ref), (2, across_ref), (3, previous_ref)):
        rows = pl.ds(pl.multiple_of(lax.rem(me_ref[0] + shift, 4) * 64, 64), 64)
        value = product(w_high[rows, :], w_low[rows, :], high_ref[...], low_ref[...])
        out[...] = value.reshape(out.shape)


def send_parts(me, w_high, w_low, high, low):
    columns = high.shape[-1]
    return pl.pallas_call(
        send_kernel,
        in_specs=[SMEM] + [FULL] * 4,
        out_specs=[FULL] * 3,
        out_shape=[jax.ShapeDtypeStruct((8, 8, columns), jnp.float32)] * 3,
        compiler_params=params(),
    )(me, w_high, w_low, high, low)


def own_kernel(me_ref, w_high, w_low, high_ref, low_ref, out):
    rows = pl.ds(pl.multiple_of(me_ref[0] * 64, 64), 64)
    value = product(w_high[rows, :], w_low[rows, :], high_ref[...], low_ref[...])
    out[...] = value.reshape(out.shape)


def own_part(me, w_high, w_low, high, low):
    return pl.pallas_call(
        own_kernel,
        in_specs=[SMEM] + [FULL] * 4,
        out_specs=FULL,
        out_shape=jax.ShapeDtypeStruct((8, 8, high.shape[-1]), jnp.float32),
        compiler_params=params(),
    )(me, w_high, w_low, high, low)


def assemble_kernel(me_ref, *refs):
    parts, out = refs[:-1], refs[-1]
    for back, part in enumerate(parts):
        out[:, lax.rem(me_ref[0] + 4 - back, 4)] = part[...]


def assemble(me, *parts):
    count, rows, columns = parts[0].shape
    step = 2
    return pl.pallas_call(
        assemble_kernel,
        grid=(count // step,),
        in_specs=[SMEM] + [pl.BlockSpec((step, rows, columns), lambda i: (i, 0, 0))] * 4,
        out_specs=pl.BlockSpec((step, 4, rows, columns), lambda i: (i, 0, 0, 0)),
        out_shape=jax.ShapeDtypeStruct((count, 4, rows, columns), jnp.float32),
        compiler_params=params(),
    )(me, *parts)


def shifted(block, shift):
    return lax.ppermute(block, "vec", [(i, (i + shift) % 4) for i in range(4)])


def exchange(blocks):
    moved = {shift: shifted(blocks[shift], shift) for shift in (2, 1, 3)}
    return [blocks[0], moved[1], moved[2], moved[3]]


def all_terms(copies):
    return lax.all_to_all(copies, ("rows", "vec"), 0, 0, tiled=True)


CHUNKS = (2, 6)


def per_device(lattice_state, constant_field, tangents):
    me = lax.axis_index("vec").astype(jnp.int32).reshape(1)
    rows, columns = lattice_state.shape[1:]
    scale = math.sqrt(2.0 * rows * lax.axis_size("rows") * columns)
    fields = jnp.stack([lattice_state, constant_field])
    first = jnp.concatenate([fields, tangents[: CHUNKS[0]]], axis=0)
    ahead = neighbours(*edges(first))
    ahead, rest = lax.optimization_barrier((ahead, edges(tangents[CHUNKS[0] :])))
    halos = [ahead, neighbours(*rest)]
    twice, next_state = pl.pallas_call(
        lattice_kernel,
        in_specs=[FULL] * 4,
        out_specs=[FULL] * 2,
        out_shape=[
            jax.ShapeDtypeStruct((STEPS, 2, rows + 2 * HALO, columns), jnp.float32),
            jax.ShapeDtypeStruct((2, rows, columns), jnp.float32),
        ],
        compiler_params=params(),
    )(lattice_state, constant_field, *halos[0])
    pieces, start = [], 0
    for count, halo in zip(CHUNKS, halos):
        if pieces:
            halo, blocks = lax.optimization_barrier((halo, blocks))
        blocks = push(me, tangents, halo, twice, start, count)
        if pieces:
            blocks, pieces = lax.optimization_barrier((blocks, pieces))
        pieces += exchange(blocks)
        start += count
    high, low, copies = inner_products(me, pieces, len(CHUNKS))
    growth, w_high, w_low = factorise(all_terms(copies), scale)
    following, across, previous = send_parts(me, w_high, w_low, high, low)
    across = shifted(across, 2)
    before = shifted(following, 1)
    after = shifted(previous, 3)
    own = own_part(me, w_high, w_low, high, low)
    basis = assemble(me, own, before, across, after)
    return (next_state, basis.reshape(tangents.shape), growth.reshape(NV))


def solution(mesh):
    return jax.shard_map(
        per_device,
        mesh=mesh,
        in_specs=(P(None, "rows", None), P(None, "rows", None), P("vec", None, "rows", None)),
        out_specs=(P(None, "rows", None), P("vec", None, "rows", None), P()),
        check_vma=False,
    )
```

```python
import math

import jax
import jax.numpy as jnp
from jax import lax
from jax.experimental import pallas as pl
from jax.experimental.pallas import tpu as pltpu
from jax.sharding import PartitionSpec as P

NV = 32
STEPS = 3
COUPLING = 0.35
HALO = 4
VMEM = 24 * 1024 * 1024
HIGHEST = lax.Precision.HIGHEST
FULL = pl.BlockSpec(memory_space=pltpu.VMEM)
SMEM = pl.BlockSpec(memory_space=pltpu.SMEM)


def params():
    return pltpu.CompilerParams(vmem_limit_bytes=VMEM)


def edges(block):
    last = lax.slice_in_dim(block, block.shape[2] - HALO, None, axis=2)
    return last, lax.slice_in_dim(block, 0, HALO, axis=2)


def neighbours(last, first):
    count = lax.axis_size("rows")
    forward = [(i, (i + 1) % count) for i in range(count)]
    backward = [(target, source) for source, target in forward]
    above = lax.ppermute(last, "rows", forward)
    below = lax.ppermute(first, "rows", backward)
    return below, above


def mix(field):
    rows, columns = field.shape
    beside = (
        pltpu.roll(field, 1, 0)
        + pltpu.roll(field, rows - 1, 0)
        + pltpu.roll(field, 1, 1)
        + pltpu.roll(field, columns - 1, 1)
    )
    return (1.0 - COUPLING) * field + (COUPLING / 4.0) * beside


def ring(block, below, above):
    return jnp.concatenate([block, below, above], axis=0)


def lattice_kernel(z_ref, c_ref, below_ref, above_ref, twice_ref, next_ref):
    real, imag = (ring(z_ref[i], below_ref[0, i], above_ref[0, i]) for i in range(2))
    const_real, const_imag = (ring(c_ref[i], below_ref[1, i], above_ref[1, i]) for i in range(2))
    for step in range(STEPS):
        twice_ref[step, 0] = 2.0 * real
        twice_ref[step, 1] = 2.0 * imag
        map_real = real * real - imag * imag + const_real
        map_imag = 2.0 * real * imag + const_imag
        real, imag = mix(map_real), mix(map_imag)
    rows = z_ref.shape[1]
    next_ref[0] = real[:rows]
    next_ref[1] = imag[:rows]


def tangent_kernel(me_ref, u_ref, below_ref, above_ref, twice_ref, *rest):
    outs, slabs = rest[:-1], rest[-1]
    real, imag = (ring(u_ref[0, i], below_ref[0, i], above_ref[0, i]) for i in range(2))
    for step in range(STEPS):
        z_real, z_imag = twice_ref[step, 0], twice_ref[step, 1]
        push_real = z_real * real - z_imag * imag
        push_imag = z_real * imag + z_imag * real
        real, imag = mix(push_real), mix(push_imag)
    slabs[0] = real[:8]
    slabs[1] = real[8:16]
    slabs[2] = imag[:8]
    slabs[3] = imag[8:16]
    for shift, out in enumerate(outs):
        out[0] = slabs[lax.rem(me_ref[0] + shift, 4)]


def push(me, vectors, halo, twice, start, count):
    columns = vectors.shape[-1]
    skip = halo[0].shape[0] - count
    return pl.pallas_call(
        tangent_kernel,
        grid=(count,),
        in_specs=[
            SMEM,
            pl.BlockSpec((1, 2, 16, columns), lambda i: (start + i, 0, 0, 0)),
            pl.BlockSpec((1, 2, HALO, columns), lambda i: (skip + i, 0, 0, 0)),
            pl.BlockSpec((1, 2, HALO, columns), lambda i: (skip + i, 0, 0, 0)),
            FULL,
        ],
        out_specs=[pl.BlockSpec((1, 8, columns), lambda i: (i, 0, 0))] * 4,
        out_shape=[jax.ShapeDtypeStruct((count, 8, columns), jnp.float32)] * 4,
        scratch_shapes=[pltpu.VMEM((4, 8, columns), jnp.float32)],
        compiler_params=params(),
        cost_estimate=pl.CostEstimate(
            flops=count * 30_000_000, bytes_accessed=count * 6_000_000, transcendentals=0
        ),
    )(me, pltpu.with_memory_space_constraint(vectors, pltpu.HBM), *halo, twice)


def same_row(shape, period):
    return lax.rem(lax.broadcasted_iota(jnp.int32, shape, 0), period) == lax.rem(
        lax.broadcasted_iota(jnp.int32, shape, 1), period
    )


def owner(shape, group):
    row = lax.broadcasted_iota(jnp.int32, shape, 0)
    column = lax.broadcasted_iota(jnp.int32, shape, 1)
    return jnp.where(row == lax.div(column, group), 1.0, 0.0)


def split(value):
    high = value.astype(jnp.bfloat16)
    return high, (value - high.astype(jnp.float32)).astype(jnp.bfloat16)


def gram_kernel(chunks, me_ref, *refs):
    pieces = refs[: 4 * chunks]
    high_ref, low_ref, gram_ref = refs[4 * chunks :]
    offset = 0
    for chunk in range(chunks):
        count, rows, columns = pieces[4 * chunk].shape
        for shift in range(4):
            source = lax.rem(me_ref[0] + 4 - shift, 4)
            start = pl.multiple_of(source * 64 + offset, 16)
            high, low = split(pieces[4 * chunk + shift][...].reshape(count * rows, columns))
            high_ref[pl.ds(start, count * rows), :] = high
            low_ref[pl.ds(start, count * rows), :] = low
        offset += count * rows
    high = high_ref[...]
    low = low_ref[...]
    last = (((1,), (1,)), ((), ()))
    main = lax.dot_general(high, high, last, preferred_element_type=jnp.float32)
    rest = lax.dot_general(high, low, last, preferred_element_type=jnp.float32)
    full = main + (rest + rest.T)
    full = jnp.where(same_row(full.shape, 8), full, 0.0)
    left = full.reshape(NV, 8, 8 * NV).sum(1)
    gram = lax.dot_general(
        left, owner((NV, 8 * NV), 8), last, precision=HIGHEST, preferred_element_type=jnp.float32
    )
    packed = jnp.concatenate([gram[8 * i : 8 * i + 8] for i in range(4)], axis=1)
    copies = gram_ref.shape[0] // 8
    gram_ref[...] = jnp.broadcast_to(packed[None], (copies, 8, 4 * NV)).reshape(gram_ref.shape)


def inner_products(me, pieces, chunks):
    columns = pieces[0].shape[-1]
    devices = lax.axis_size("rows") * lax.axis_size("vec")
    return pl.pallas_call(
        lambda *refs: gram_kernel(chunks, *refs),
        in_specs=[SMEM] + [FULL] * len(pieces),
        out_specs=[FULL] * 3,
        out_shape=[
            jax.ShapeDtypeStruct((8 * NV, columns), jnp.bfloat16),
            jax.ShapeDtypeStruct((8 * NV, columns), jnp.bfloat16),
            jax.ShapeDtypeStruct((8 * devices, 4 * NV), jnp.float32),
        ],
        compiler_params=params(),
    )(me, *pieces)


def factor_kernel(scale, terms_ref, growth_ref, high_ref, low_ref):
    row = lax.broadcasted_iota(jnp.int32, (NV, 2 * NV), 0)
    column = lax.broadcasted_iota(jnp.int32, (NV, 2 * NV), 1)
    spread = jnp.where(row == column, 1.0, 0.0)
    last = (((1,), (0,)), ((), ()))
    packed = jnp.sum(terms_ref[...].reshape(terms_ref.shape[0] // 8, 8, 4 * NV), axis=0)
    gram = jnp.concatenate([packed[:, NV * i : NV * i + NV] for i in range(4)], axis=0)
    work = jnp.where(column == row + NV, 1.0, 0.0) + lax.dot_general(
        gram, spread, last, precision=HIGHEST, preferred_element_type=jnp.float32
    )
    for k in range(NV):
        pivot_row = work[k : k + 1, :]
        pivot = pivot_row[:, k : k + 1]
        inverse = lax.rsqrt(pivot)
        inverse = inverse * (1.5 - 0.5 * pivot * inverse * inverse)
        scaled = pivot_row * inverse
        factor = work[:, k : k + 1] * inverse
        work = jnp.where(row > k, work - factor * scaled, jnp.where(row == k, scaled, work))
    diagonal = jnp.sum(jnp.where(column == row, work, 0.0), axis=0, keepdims=True)
    growth_ref[...] = jnp.log(diagonal[:, :NV] / scale)
    inverse = work[:, NV:] * scale
    wide = lax.dot_general(
        inverse,
        owner((NV, 8 * NV), 8),
        last,
        precision=HIGHEST,
        preferred_element_type=jnp.float32,
    )
    tall = jnp.broadcast_to(wide[:, None, :], (NV, 8, 8 * NV)).reshape(8 * NV, 8 * NV)
    weights = jnp.where(same_row(tall.shape, 8), tall, 0.0)
    high = weights.astype(jnp.bfloat16)
    high_ref[...] = high
    low_ref[...] = (weights - high.astype(jnp.float32)).astype(jnp.bfloat16)


def factorise(terms, scale):
    return pl.pallas_call(
        lambda *refs: factor_kernel(scale, *refs),
        in_specs=[FULL],
        out_specs=[FULL] * 3,
        out_shape=[jax.ShapeDtypeStruct((1, NV), jnp.float32)]
        + [jax.ShapeDtypeStruct((8 * NV, 8 * NV), jnp.bfloat16)] * 2,
        compiler_params=params(),
    )(terms)


def product(w_high, w_low, high, low):
    value = jnp.dot(w_high, high, preferred_element_type=jnp.float32)
    value += jnp.dot(w_high, low, preferred_element_type=jnp.float32)
    return value + jnp.dot(w_low, high, preferred_element_type=jnp.float32)


def send_kernel(me_ref, w_high, w_low, high_ref, low_ref, next_ref, across_ref, previous_ref):
    for shift, out in ((1, next_ref), (2, across_ref), (3, previous_ref)):
        rows = pl.ds(pl.multiple_of(lax.rem(me_ref[0] + shift, 4) * 64, 64), 64)
        skip = high_ref.shape[1] - out.shape[2]
        value = product(w_high[rows, :], w_low[rows, :], high_ref[:, skip:], low_ref[:, skip:])
        out[...] = value.reshape(out.shape)


def send_parts(me, w_high, w_low, high, low):
    columns = high.shape[-1]
    return pl.pallas_call(
        send_kernel,
        in_specs=[SMEM] + [FULL] * 4,
        out_specs=[FULL] * 3,
        out_shape=[
            jax.ShapeDtypeStruct((8, 8, width), jnp.float32)
            for width in (columns, columns - NEAR, columns)
        ],
        compiler_params=params(),
    )(me, w_high, w_low, high, low)


def own_kernel(me_ref, w_high, w_low, high_ref, low_ref, *refs):
    pieces, (own_ref, far_ref, far_high, far_low) = refs[:-4], refs[-4:]
    me = me_ref[0]
    for back, piece in enumerate(pieces):
        start = pl.multiple_of(lax.rem(me + 4 - back, 4) * 64, 64)
        high, low = split(piece[...].reshape(64, piece.shape[2]))
        far_high[pl.ds(start, 64), :] = high
        far_low[pl.ds(start, 64), :] = low
    rows = pl.ds(pl.multiple_of(me * 64, 64), 64)
    own_high, own_low = w_high[rows, :], w_low[rows, :]
    own_ref[...] = product(own_high, own_low, high_ref[...], low_ref[...]).reshape(own_ref.shape)
    far_ref[...] = product(own_high, own_low, far_high[...], far_low[...]).reshape(far_ref.shape)


def own_parts(me, w_high, w_low, high, low, pieces):
    columns = high.shape[-1]
    return pl.pallas_call(
        own_kernel,
        in_specs=[SMEM] + [FULL] * (4 + len(pieces)),
        out_specs=[FULL] * 2,
        out_shape=[
            jax.ShapeDtypeStruct((8, 8, width), jnp.float32) for width in (columns, NEAR)
        ],
        scratch_shapes=[pltpu.VMEM((8 * NV, NEAR), jnp.bfloat16)] * 2,
        compiler_params=params(),
    )(me, w_high, w_low, high, low, *pieces)


def assemble_kernel(me_ref, own_ref, far_ref, before_ref, across_ref, after_ref, out):
    me = me_ref[0]
    opposite_slab = lax.rem(me + 2, 4)
    out[:, me] = own_ref[...]
    out[:, opposite_slab, :, :NEAR] = far_ref[...]
    out[:, opposite_slab, :, NEAR:] = across_ref[...]
    out[:, lax.rem(me + 3, 4)] = before_ref[...]
    out[:, lax.rem(me + 1, 4)] = after_ref[...]


def assemble(me, own, before, across, after):
    parts = (*own, before, across, after)
    count, rows, columns = before.shape
    step = 2
    return pl.pallas_call(
        assemble_kernel,
        grid=(count // step,),
        in_specs=[SMEM]
        + [pl.BlockSpec((step, rows, part.shape[2]), lambda i: (i, 0, 0)) for part in parts],
        out_specs=pl.BlockSpec((step, 4, rows, columns), lambda i: (i, 0, 0, 0)),
        out_shape=jax.ShapeDtypeStruct((count, 4, rows, columns), jnp.float32),
        compiler_params=params(),
    )(me, *parts)


def shifted(block, shift):
    return lax.ppermute(block, "vec", [(i, (i + shift) % 4) for i in range(4)])


def exchange(blocks):
    moved = {shift: shifted(blocks[shift], shift) for shift in (2, 1, 3)}
    return [blocks[0], moved[1], moved[2], moved[3]]


def opposite(blocks):
    one = lax.ppermute(blocks[3], "vec", [(0, 1), (1, 2), (2, 3)])
    two = lax.ppermute(blocks[0], "vec", [(0, 2), (1, 3)])
    three = lax.ppermute(blocks[1], "vec", [(0, 3)])
    return [blocks[2], one, two, three]


def all_terms(copies):
    return lax.all_to_all(copies, ("rows", "vec"), 0, 0, tiled=True)


CHUNKS = (2, 6)
NEAR = 2048


def per_device(lattice_state, constant_field, tangents):
    me = lax.axis_index("vec").astype(jnp.int32).reshape(1)
    rows, columns = lattice_state.shape[1:]
    scale = math.sqrt(2.0 * rows * lax.axis_size("rows") * columns)
    fields = jnp.stack([lattice_state, constant_field])
    first = jnp.concatenate([fields, tangents[: CHUNKS[0]]], axis=0)
    ahead = neighbours(*edges(first))
    ahead, rest = lax.optimization_barrier((ahead, edges(tangents[CHUNKS[0] :])))
    halos = [ahead, neighbours(*rest)]
    twice, next_state = pl.pallas_call(
        lattice_kernel,
        in_specs=[FULL] * 4,
        out_specs=[FULL] * 2,
        out_shape=[
            jax.ShapeDtypeStruct((STEPS, 2, rows + 2 * HALO, columns), jnp.float32),
            jax.ShapeDtypeStruct((2, rows, columns), jnp.float32),
        ],
        compiler_params=params(),
    )(lattice_state, constant_field, *halos[0])
    pieces, local, start = [], [], 0
    for count, halo in zip(CHUNKS, halos):
        if pieces:
            halo, blocks = lax.optimization_barrier((halo, blocks))
        blocks = push(me, tangents, halo, twice, start, count)
        if pieces:
            blocks, pieces = lax.optimization_barrier((blocks, pieces))
        local.append(blocks)
        pieces += exchange(blocks)
        start += count
    slabs = [
        jnp.concatenate([blocks[shift][:, :, :NEAR] for blocks in local], axis=0)
        for shift in range(4)
    ]
    slabs, pieces[5] = lax.optimization_barrier((slabs, pieces[5]))
    far = opposite(slabs)
    high, low, copies = inner_products(me, pieces, len(CHUNKS))
    terms, far = lax.optimization_barrier((all_terms(copies), far))
    growth, w_high, w_low = factorise(terms, scale)
    following, across, previous = send_parts(me, w_high, w_low, high, low)
    across = shifted(across, 2)
    before = shifted(following, 1)
    after = shifted(previous, 3)
    own = own_parts(me, w_high, w_low, high, low, far)
    basis = assemble(me, own, before, across, after)
    return (next_state, basis.reshape(tangents.shape), growth.reshape(NV))


def solution(mesh):
    return jax.shard_map(
        per_device,
        mesh=mesh,
        in_specs=(P(None, "rows", None), P(None, "rows", None), P("vec", None, "rows", None)),
        out_specs=(P(None, "rows", None), P("vec", None, "rows", None), P()),
        check_vma=False,
    )
```

```python
import math

import jax
import jax.numpy as jnp
from jax import lax
from jax.experimental import pallas as pl
from jax.experimental.pallas import tpu as pltpu
from jax.sharding import PartitionSpec as P

NV = 32
STEPS = 3
COUPLING = 0.35
HALO = 4
VMEM = 24 * 1024 * 1024
HIGHEST = lax.Precision.HIGHEST
FULL = pl.BlockSpec(memory_space=pltpu.VMEM)
SMEM = pl.BlockSpec(memory_space=pltpu.SMEM)
HBM = pl.BlockSpec(memory_space=pltpu.HBM)


def params():
    return pltpu.CompilerParams(vmem_limit_bytes=VMEM)


def edges(block):
    last = lax.slice_in_dim(block, block.shape[2] - HALO, None, axis=2)
    return last, lax.slice_in_dim(block, 0, HALO, axis=2)


def neighbours(last, first):
    count = lax.axis_size("rows")
    forward = [(i, (i + 1) % count) for i in range(count)]
    backward = [(target, source) for source, target in forward]
    above = lax.ppermute(last, "rows", forward)
    below = lax.ppermute(first, "rows", backward)
    return below, above


def mix(field):
    rows, columns = field.shape
    beside = (
        pltpu.roll(field, 1, 0)
        + pltpu.roll(field, rows - 1, 0)
        + pltpu.roll(field, 1, 1)
        + pltpu.roll(field, columns - 1, 1)
    )
    return (1.0 - COUPLING) * field + (COUPLING / 4.0) * beside


def ring(block, below, above):
    return jnp.concatenate([block, below, above], axis=0)


def lattice_kernel(z_ref, c_ref, below_ref, above_ref, twice_ref, next_ref):
    real, imag = (ring(z_ref[i], below_ref[0, i], above_ref[0, i]) for i in range(2))
    const_real, const_imag = (ring(c_ref[i], below_ref[1, i], above_ref[1, i]) for i in range(2))
    for step in range(STEPS):
        twice_ref[step, 0] = 2.0 * real
        twice_ref[step, 1] = 2.0 * imag
        map_real = real * real - imag * imag + const_real
        map_imag = 2.0 * real * imag + const_imag
        real, imag = mix(map_real), mix(map_imag)
    rows = z_ref.shape[1]
    next_ref[0] = real[:rows]
    next_ref[1] = imag[:rows]


def tangent_kernel(me_ref, u_ref, below_ref, above_ref, twice_ref, *rest):
    outs, slabs = rest[:-1], rest[-1]
    real, imag = (ring(u_ref[0, i], below_ref[0, i], above_ref[0, i]) for i in range(2))
    for step in range(STEPS):
        z_real, z_imag = twice_ref[step, 0], twice_ref[step, 1]
        push_real = z_real * real - z_imag * imag
        push_imag = z_real * imag + z_imag * real
        real, imag = mix(push_real), mix(push_imag)
    slabs[0] = real[:8]
    slabs[1] = real[8:16]
    slabs[2] = imag[:8]
    slabs[3] = imag[8:16]
    for shift, out in enumerate(outs):
        out[0] = slabs[lax.rem(me_ref[0] + shift, 4)]


def push(me, vectors, halo, twice, start, count):
    columns = vectors.shape[-1]
    skip = halo[0].shape[0] - count
    return pl.pallas_call(
        tangent_kernel,
        grid=(count,),
        in_specs=[
            SMEM,
            pl.BlockSpec((1, 2, 16, columns), lambda i: (start + i, 0, 0, 0)),
            pl.BlockSpec((1, 2, HALO, columns), lambda i: (skip + i, 0, 0, 0)),
            pl.BlockSpec((1, 2, HALO, columns), lambda i: (skip + i, 0, 0, 0)),
            FULL,
        ],
        out_specs=[pl.BlockSpec((1, 8, columns), lambda i: (i, 0, 0))] * 4,
        out_shape=[jax.ShapeDtypeStruct((count, 8, columns), jnp.float32)] * 4,
        scratch_shapes=[pltpu.VMEM((4, 8, columns), jnp.float32)],
        compiler_params=params(),
        cost_estimate=pl.CostEstimate(
            flops=count * 30_000_000, bytes_accessed=count * 6_000_000, transcendentals=0
        ),
    )(me, pltpu.with_memory_space_constraint(vectors, pltpu.HBM), *halo, twice)


def same_row(shape, period):
    return lax.rem(lax.broadcasted_iota(jnp.int32, shape, 0), period) == lax.rem(
        lax.broadcasted_iota(jnp.int32, shape, 1), period
    )


def owner(shape, group):
    row = lax.broadcasted_iota(jnp.int32, shape, 0)
    column = lax.broadcasted_iota(jnp.int32, shape, 1)
    return jnp.where(row == lax.div(column, group), 1.0, 0.0)


def split(value):
    high = value.astype(jnp.bfloat16)
    return high, (value - high.astype(jnp.float32)).astype(jnp.bfloat16)


def gram_kernel(chunks, me_ref, *refs):
    pieces = refs[: 4 * chunks]
    high_ref, low_ref, gram_ref = refs[4 * chunks :]
    offset = 0
    for chunk in range(chunks):
        count, rows, columns = pieces[4 * chunk].shape
        for shift in range(4):
            source = lax.rem(me_ref[0] + 4 - shift, 4)
            start = pl.multiple_of(source * 64 + offset, 16)
            high, low = split(pieces[4 * chunk + shift][...].reshape(count * rows, columns))
            high_ref[pl.ds(start, count * rows), :] = high
            low_ref[pl.ds(start, count * rows), :] = low
        offset += count * rows
    high = high_ref[...]
    low = low_ref[...]
    last = (((1,), (1,)), ((), ()))
    main = lax.dot_general(high, high, last, preferred_element_type=jnp.float32)
    rest = lax.dot_general(high, low, last, preferred_element_type=jnp.float32)
    full = main + (rest + rest.T)
    full = jnp.where(same_row(full.shape, 8), full, 0.0)
    left = full.reshape(NV, 8, 8 * NV).sum(1)
    gram = lax.dot_general(
        left, owner((NV, 8 * NV), 8), last, precision=HIGHEST, preferred_element_type=jnp.float32
    )
    packed = jnp.concatenate([gram[8 * i : 8 * i + 8] for i in range(4)], axis=1)
    copies = gram_ref.shape[0] // 8
    gram_ref[...] = jnp.broadcast_to(packed[None], (copies, 8, 4 * NV)).reshape(gram_ref.shape)


def inner_products(me, pieces, chunks):
    columns = pieces[0].shape[-1]
    devices = lax.axis_size("rows") * lax.axis_size("vec")
    return pl.pallas_call(
        lambda *refs: gram_kernel(chunks, *refs),
        in_specs=[SMEM] + [FULL] * len(pieces),
        out_specs=[FULL] * 3,
        out_shape=[
            jax.ShapeDtypeStruct((8 * NV, columns), jnp.bfloat16),
            jax.ShapeDtypeStruct((8 * NV, columns), jnp.bfloat16),
            jax.ShapeDtypeStruct((8 * devices, 4 * NV), jnp.float32),
        ],
        compiler_params=params(),
    )(me, *pieces)


def factor_kernel(
    scale,
    me_ref,
    terms_ref,
    high_ref,
    low_ref,
    growth_ref,
    w_high,
    w_low,
    next_ref,
    across_ref,
    previous_ref,
):
    row = lax.broadcasted_iota(jnp.int32, (NV, 2 * NV), 0)
    column = lax.broadcasted_iota(jnp.int32, (NV, 2 * NV), 1)
    spread = jnp.where(row == column, 1.0, 0.0)
    last = (((1,), (0,)), ((), ()))
    packed = jnp.sum(terms_ref[...].reshape(terms_ref.shape[0] // 8, 8, 4 * NV), axis=0)
    gram = jnp.concatenate([packed[:, NV * i : NV * i + NV] for i in range(4)], axis=0)
    work = jnp.where(column == row + NV, 1.0, 0.0) + lax.dot_general(
        gram, spread, last, precision=HIGHEST, preferred_element_type=jnp.float32
    )
    for k in range(NV):
        pivot_row = work[k : k + 1, :]
        pivot = pivot_row[:, k : k + 1]
        inverse = lax.rsqrt(pivot)
        inverse = inverse * (1.5 - 0.5 * pivot * inverse * inverse)
        scaled = pivot_row * inverse
        factor = work[:, k : k + 1] * inverse
        work = jnp.where(row > k, work - factor * scaled, jnp.where(row == k, scaled, work))
    diagonal = jnp.sum(jnp.where(column == row, work, 0.0), axis=0, keepdims=True)
    growth_ref[...] = jnp.log(diagonal[:, :NV] / scale)
    inverse = work[:, NV:] * scale
    wide = lax.dot_general(
        inverse,
        owner((NV, 8 * NV), 8),
        last,
        precision=HIGHEST,
        preferred_element_type=jnp.float32,
    )
    tall = jnp.broadcast_to(wide[:, None, :], (NV, 8, 8 * NV)).reshape(8 * NV, 8 * NV)
    weights = jnp.where(same_row(tall.shape, 8), tall, 0.0)
    high = weights.astype(jnp.bfloat16)
    w_high[...] = high
    w_low[...] = (weights - high.astype(jnp.float32)).astype(jnp.bfloat16)
    for shift, out in ((1, next_ref), (2, across_ref), (3, previous_ref)):
        rows = pl.ds(pl.multiple_of(lax.rem(me_ref[0] + shift, 4) * 64, 64), 64)
        skip = high_ref.shape[1] - out.shape[2]
        value = product(w_high[rows, :], w_low[rows, :], high_ref[:, skip:], low_ref[:, skip:])
        out[...] = value.reshape(out.shape)


def factorise(me, terms, high, low, scale):
    columns = high.shape[-1]
    return pl.pallas_call(
        lambda *refs: factor_kernel(scale, *refs),
        in_specs=[SMEM] + [FULL] * 3,
        out_specs=[FULL] * 6,
        out_shape=[jax.ShapeDtypeStruct((1, NV), jnp.float32)]
        + [jax.ShapeDtypeStruct((8 * NV, 8 * NV), jnp.bfloat16)] * 2
        + [
            jax.ShapeDtypeStruct((8, 8, width), jnp.float32)
            for width in (columns, columns - NEAR, columns)
        ],
        compiler_params=params(),
    )(me, terms, high, low)


def product(w_high, w_low, high, low):
    value = jnp.dot(w_high, high, preferred_element_type=jnp.float32)
    value += jnp.dot(w_high, low, preferred_element_type=jnp.float32)
    return value + jnp.dot(w_low, high, preferred_element_type=jnp.float32)


def own_kernel(me_ref, w_high, w_low, high_ref, low_ref, *refs):
    pieces, (out, own_ref, far_ref, far_high, far_low, sems) = refs[:-6], refs[-6:]
    me = me_ref[0]
    for back, piece in enumerate(pieces):
        start = pl.multiple_of(lax.rem(me + 4 - back, 4) * 64, 64)
        high, low = split(piece[...].reshape(64, piece.shape[2]))
        far_high[pl.ds(start, 64), :] = high
        far_low[pl.ds(start, 64), :] = low
    rows = pl.ds(pl.multiple_of(me * 64, 64), 64)
    own_high, own_low = w_high[rows, :], w_low[rows, :]
    own_ref[...] = product(own_high, own_low, high_ref[...], low_ref[...]).reshape(own_ref.shape)
    own_copy = pltpu.make_async_copy(own_ref, out.at[:, me], sems.at[0])
    own_copy.start()
    far_ref[...] = product(own_high, own_low, far_high[...], far_low[...]).reshape(far_ref.shape)
    far_copy = pltpu.make_async_copy(
        far_ref, out.at[:, lax.rem(me + 2, 4), :, pl.ds(0, NEAR)], sems.at[1]
    )
    far_copy.start()
    own_copy.wait()
    far_copy.wait()


def own_parts(me, w_high, w_low, high, low, pieces):
    columns = high.shape[-1]
    return pl.pallas_call(
        own_kernel,
        in_specs=[SMEM] + [FULL] * (4 + len(pieces)),
        out_specs=HBM,
        out_shape=jax.ShapeDtypeStruct((8, 4, 8, columns), jnp.float32),
        scratch_shapes=[
            pltpu.VMEM((8, 8, columns), jnp.float32),
            pltpu.VMEM((8, 8, NEAR), jnp.float32),
            pltpu.VMEM((8 * NV, NEAR), jnp.bfloat16),
            pltpu.VMEM((8 * NV, NEAR), jnp.bfloat16),
            pltpu.SemaphoreType.DMA((2,)),
        ],
        compiler_params=params(),
    )(me, w_high, w_low, high, low, *pieces)


def assemble_kernel(me_ref, own_ref, before_ref, across_ref, after_ref, out, sems):
    me = me_ref[0]
    width = across_ref.shape[2]
    far = out.at[:, lax.rem(me + 2, 4), :, pl.ds(out.shape[3] - width, width)]
    copies = [
        pltpu.make_async_copy(before_ref, out.at[:, lax.rem(me + 3, 4)], sems.at[0]),
        pltpu.make_async_copy(after_ref, out.at[:, lax.rem(me + 1, 4)], sems.at[1]),
        pltpu.make_async_copy(across_ref, far, sems.at[2]),
    ]
    for copy in copies:
        copy.start()
    for copy in copies:
        copy.wait()


def assemble(me, own, before, across, after):
    return pl.pallas_call(
        assemble_kernel,
        in_specs=[SMEM, HBM] + [pl.BlockSpec(memory_space=pl.ANY)] * 3,
        out_specs=HBM,
        out_shape=jax.ShapeDtypeStruct(own.shape, own.dtype),
        scratch_shapes=[pltpu.SemaphoreType.DMA((3,))],
        input_output_aliases={1: 0},
        compiler_params=params(),
    )(me, own, before, across, after)


def shifted(block, shift):
    return lax.ppermute(block, "vec", [(i, (i + shift) % 4) for i in range(4)])


def exchange(blocks):
    moved = {shift: shifted(blocks[shift], shift) for shift in (2, 1, 3)}
    return [blocks[0], moved[1], moved[2], moved[3]]


def opposite(blocks):
    one = lax.ppermute(blocks[3], "vec", [(0, 1), (1, 2), (2, 3)])
    two = lax.ppermute(blocks[0], "vec", [(0, 2), (1, 3)])
    three = lax.ppermute(blocks[1], "vec", [(0, 3)])
    return [blocks[2], one, two, three]


def all_terms(copies):
    return lax.all_to_all(copies, ("rows", "vec"), 0, 0, tiled=True)


CHUNKS = (2, 6)
NEAR = 2048


def per_device(lattice_state, constant_field, tangents):
    me = lax.axis_index("vec").astype(jnp.int32).reshape(1)
    rows, columns = lattice_state.shape[1:]
    scale = math.sqrt(2.0 * rows * lax.axis_size("rows") * columns)
    sources = (lattice_state[None], constant_field[None], tangents[: CHUNKS[0]])
    ahead = neighbours(
        *(jnp.concatenate(parts, axis=0) for parts in zip(*(edges(part) for part in sources)))
    )
    ahead, rest = lax.optimization_barrier((ahead, edges(tangents[CHUNKS[0] :])))
    halos = [ahead, neighbours(*rest)]
    twice, next_state = pl.pallas_call(
        lattice_kernel,
        in_specs=[FULL] * 4,
        out_specs=[FULL] * 2,
        out_shape=[
            jax.ShapeDtypeStruct((STEPS, 2, rows + 2 * HALO, columns), jnp.float32),
            jax.ShapeDtypeStruct((2, rows, columns), jnp.float32),
        ],
        compiler_params=params(),
    )(lattice_state, constant_field, *halos[0])
    pieces, local, start = [], [], 0
    for count, halo in zip(CHUNKS, halos):
        if pieces:
            halo, blocks = lax.optimization_barrier((halo, blocks))
        blocks = push(me, tangents, halo, twice, start, count)
        if pieces:
            blocks, pieces = lax.optimization_barrier((blocks, pieces))
        local.append(blocks)
        pieces += exchange(blocks)
        start += count
    slabs = [
        jnp.concatenate([blocks[shift][:, :, :NEAR] for blocks in local], axis=0)
        for shift in range(4)
    ]
    slabs, pieces[5] = lax.optimization_barrier((slabs, pieces[5]))
    far = opposite(slabs)
    high, low, copies = inner_products(me, pieces, len(CHUNKS))
    terms, far = lax.optimization_barrier((all_terms(copies), far))
    growth, w_high, w_low, following, across, previous = factorise(me, terms, high, low, scale)
    across = shifted(across, 2)
    before = shifted(following, 1)
    after = shifted(previous, 3)
    own = own_parts(me, w_high, w_low, high, low, far)
    basis = assemble(me, own, before, across, after)
    return (next_state, basis.reshape(tangents.shape), growth.reshape(NV))


def solution(mesh):
    return jax.shard_map(
        per_device,
        mesh=mesh,
        in_specs=(P(None, "rows", None), P(None, "rows", None), P("vec", None, "rows", None)),
        out_specs=(P(None, "rows", None), P("vec", None, "rows", None), P()),
        check_vma=False,
    )
```

```python
import math

import jax
import jax.numpy as jnp
from jax import lax
from jax.experimental import pallas as pl
from jax.experimental.pallas import tpu as pltpu
from jax.sharding import PartitionSpec as P

NV = 32
STEPS = 3
COUPLING = 0.35
HALO = 4
VMEM = 24 * 1024 * 1024
HIGHEST = lax.Precision.HIGHEST
FULL = pl.BlockSpec(memory_space=pltpu.VMEM)
SMEM = pl.BlockSpec(memory_space=pltpu.SMEM)
HBM = pl.BlockSpec(memory_space=pltpu.HBM)


def params():
    return pltpu.CompilerParams(vmem_limit_bytes=VMEM)


def edges(block):
    last = lax.slice_in_dim(block, block.shape[2] - HALO, None, axis=2)
    return last, lax.slice_in_dim(block, 0, HALO, axis=2)


def neighbours(last, first):
    count = lax.axis_size("rows")
    forward = [(i, (i + 1) % count) for i in range(count)]
    backward = [(target, source) for source, target in forward]
    above = lax.ppermute(last, "rows", forward)
    below = lax.ppermute(first, "rows", backward)
    return below, above


def mix(field):
    rows, columns = field.shape
    beside = (
        pltpu.roll(field, 1, 0)
        + pltpu.roll(field, rows - 1, 0)
        + pltpu.roll(field, 1, 1)
        + pltpu.roll(field, columns - 1, 1)
    )
    return (1.0 - COUPLING) * field + (COUPLING / 4.0) * beside


def ring(block, below, above):
    return jnp.concatenate([block, below, above], axis=0)


def lattice_kernel(z_ref, c_ref, below_ref, above_ref, twice_ref, next_ref):
    real, imag = (ring(z_ref[i], below_ref[0, i], above_ref[0, i]) for i in range(2))
    const_real, const_imag = (ring(c_ref[i], below_ref[1, i], above_ref[1, i]) for i in range(2))
    for step in range(STEPS):
        twice_ref[step, 0] = 2.0 * real
        twice_ref[step, 1] = 2.0 * imag
        map_real = real * real - imag * imag + const_real
        map_imag = 2.0 * real * imag + const_imag
        real, imag = mix(map_real), mix(map_imag)
    rows = z_ref.shape[1]
    next_ref[0] = real[:rows]
    next_ref[1] = imag[:rows]


def tangent_kernel(me_ref, u_ref, below_ref, above_ref, twice_ref, *rest):
    outs, slabs = rest[:-1], rest[-1]
    real, imag = (ring(u_ref[0, i], below_ref[0, i], above_ref[0, i]) for i in range(2))
    for step in range(STEPS):
        z_real, z_imag = twice_ref[step, 0], twice_ref[step, 1]
        push_real = z_real * real - z_imag * imag
        push_imag = z_real * imag + z_imag * real
        real, imag = mix(push_real), mix(push_imag)
    slabs[0] = real[:8]
    slabs[1] = real[8:16]
    slabs[2] = imag[:8]
    slabs[3] = imag[8:16]
    for shift, out in enumerate(outs):
        out[0] = slabs[lax.rem(me_ref[0] + shift, 4)]


def first_kernel(
    me_ref,
    u_ref,
    below_ref,
    above_ref,
    z_ref,
    c_ref,
    fields_below,
    fields_above,
    *rest,
):
    outs, twice_ref, next_ref, slabs = rest[:-3], *rest[-3:]

    @pl.when(pl.program_id(0) == 0)
    def _():
        lattice_kernel(z_ref, c_ref, fields_below, fields_above, twice_ref, next_ref)

    tangent_kernel(me_ref, u_ref, below_ref, above_ref, twice_ref, *outs, slabs)


def push_first(me, lattice_state, constant_field, vectors, halo, count):
    rows, columns = lattice_state.shape[1:]
    edge = pl.BlockSpec((1, 2, HALO, columns), lambda i: (2 + i, 0, 0, 0))
    fields = pl.BlockSpec((2, 2, HALO, columns), lambda i: (0, 0, 0, 0))
    *blocks, twice, next_state = pl.pallas_call(
        first_kernel,
        grid=(count,),
        in_specs=[
            SMEM,
            pl.BlockSpec((1, 2, rows, columns), lambda i: (i, 0, 0, 0)),
            edge,
            edge,
            FULL,
            FULL,
            fields,
            fields,
        ],
        out_specs=[pl.BlockSpec((1, 8, columns), lambda i: (i, 0, 0))] * 4 + [FULL] * 2,
        out_shape=[jax.ShapeDtypeStruct((count, 8, columns), jnp.float32)] * 4
        + [
            jax.ShapeDtypeStruct((STEPS, 2, rows + 2 * HALO, columns), jnp.float32),
            jax.ShapeDtypeStruct((2, rows, columns), jnp.float32),
        ],
        scratch_shapes=[pltpu.VMEM((4, 8, columns), jnp.float32)],
        compiler_params=params(),
        cost_estimate=pl.CostEstimate(
            flops=count * 45_000_000, bytes_accessed=count * 9_000_000, transcendentals=0
        ),
    )(
        me,
        pltpu.with_memory_space_constraint(vectors, pltpu.HBM),
        *halo,
        lattice_state,
        constant_field,
        *halo,
    )
    return blocks, twice, next_state


def push(me, vectors, halo, twice, start, count):
    columns = vectors.shape[-1]
    skip = halo[0].shape[0] - count
    return pl.pallas_call(
        tangent_kernel,
        grid=(count,),
        in_specs=[
            SMEM,
            pl.BlockSpec((1, 2, 16, columns), lambda i: (start + i, 0, 0, 0)),
            pl.BlockSpec((1, 2, HALO, columns), lambda i: (skip + i, 0, 0, 0)),
            pl.BlockSpec((1, 2, HALO, columns), lambda i: (skip + i, 0, 0, 0)),
            FULL,
        ],
        out_specs=[pl.BlockSpec((1, 8, columns), lambda i: (i, 0, 0))] * 4,
        out_shape=[jax.ShapeDtypeStruct((count, 8, columns), jnp.float32)] * 4,
        scratch_shapes=[pltpu.VMEM((4, 8, columns), jnp.float32)],
        compiler_params=params(),
        cost_estimate=pl.CostEstimate(
            flops=count * 30_000_000, bytes_accessed=count * 6_000_000, transcendentals=0
        ),
    )(me, pltpu.with_memory_space_constraint(vectors, pltpu.HBM), *halo, twice)


def same_row(shape, period):
    return lax.rem(lax.broadcasted_iota(jnp.int32, shape, 0), period) == lax.rem(
        lax.broadcasted_iota(jnp.int32, shape, 1), period
    )


def owner(shape, group):
    row = lax.broadcasted_iota(jnp.int32, shape, 0)
    column = lax.broadcasted_iota(jnp.int32, shape, 1)
    return jnp.where(row == lax.div(column, group), 1.0, 0.0)


def split(value):
    high = value.astype(jnp.bfloat16)
    return high, (value - high.astype(jnp.float32)).astype(jnp.bfloat16)


def gram_kernel(chunks, me_ref, *refs):
    pieces = refs[: 4 * chunks]
    high_ref, low_ref, gram_ref = refs[4 * chunks :]
    offset = 0
    for chunk in range(chunks):
        count, rows, columns = pieces[4 * chunk].shape
        for shift in range(4):
            source = lax.rem(me_ref[0] + 4 - shift, 4)
            start = pl.multiple_of(source * 64 + offset, 16)
            high, low = split(pieces[4 * chunk + shift][...].reshape(count * rows, columns))
            high_ref[pl.ds(start, count * rows), :] = high
            low_ref[pl.ds(start, count * rows), :] = low
        offset += count * rows
    high = high_ref[...]
    low = low_ref[...]
    last = (((1,), (1,)), ((), ()))
    main = lax.dot_general(high, high, last, preferred_element_type=jnp.float32)
    rest = lax.dot_general(high, low, last, preferred_element_type=jnp.float32)
    full = main + (rest + rest.T)
    full = jnp.where(same_row(full.shape, 8), full, 0.0)
    left = full.reshape(NV, 8, 8 * NV).sum(1)
    gram = lax.dot_general(
        left, owner((NV, 8 * NV), 8), last, precision=HIGHEST, preferred_element_type=jnp.float32
    )
    packed = jnp.concatenate([gram[8 * i : 8 * i + 8] for i in range(4)], axis=1)
    copies = gram_ref.shape[0] // 8
    gram_ref[...] = jnp.broadcast_to(packed[None], (copies, 8, 4 * NV)).reshape(gram_ref.shape)


def inner_products(me, pieces, chunks):
    columns = pieces[0].shape[-1]
    devices = lax.axis_size("rows") * lax.axis_size("vec")
    return pl.pallas_call(
        lambda *refs: gram_kernel(chunks, *refs),
        in_specs=[SMEM] + [FULL] * len(pieces),
        out_specs=[FULL] * 3,
        out_shape=[
            jax.ShapeDtypeStruct((8 * NV, columns), jnp.bfloat16),
            jax.ShapeDtypeStruct((8 * NV, columns), jnp.bfloat16),
            jax.ShapeDtypeStruct((8 * devices, 4 * NV), jnp.float32),
        ],
        compiler_params=params(),
    )(me, *pieces)


def factor_kernel(
    scale,
    me_ref,
    terms_ref,
    high_ref,
    low_ref,
    growth_ref,
    w_high,
    w_low,
    next_ref,
    across_ref,
    previous_ref,
):
    row = lax.broadcasted_iota(jnp.int32, (NV, 2 * NV), 0)
    column = lax.broadcasted_iota(jnp.int32, (NV, 2 * NV), 1)
    spread = jnp.where(row == column, 1.0, 0.0)
    last = (((1,), (0,)), ((), ()))
    packed = jnp.sum(terms_ref[...].reshape(terms_ref.shape[0] // 8, 8, 4 * NV), axis=0)
    gram = jnp.concatenate([packed[:, NV * i : NV * i + NV] for i in range(4)], axis=0)
    work = jnp.where(column == row + NV, 1.0, 0.0) + lax.dot_general(
        gram, spread, last, precision=HIGHEST, preferred_element_type=jnp.float32
    )
    for k in range(NV):
        pivot_row = work[k : k + 1, :]
        pivot = pivot_row[:, k : k + 1]
        inverse = lax.rsqrt(pivot)
        inverse = inverse * (1.5 - 0.5 * pivot * inverse * inverse)
        scaled = pivot_row * inverse
        factor = work[:, k : k + 1] * inverse
        work = jnp.where(row > k, work - factor * scaled, jnp.where(row == k, scaled, work))
    diagonal = jnp.sum(jnp.where(column == row, work, 0.0), axis=0, keepdims=True)
    growth_ref[...] = jnp.log(diagonal[:, :NV] / scale)
    inverse = work[:, NV:] * scale
    wide = lax.dot_general(
        inverse,
        owner((NV, 8 * NV), 8),
        last,
        precision=HIGHEST,
        preferred_element_type=jnp.float32,
    )
    tall = jnp.broadcast_to(wide[:, None, :], (NV, 8, 8 * NV)).reshape(8 * NV, 8 * NV)
    weights = jnp.where(same_row(tall.shape, 8), tall, 0.0)
    high = weights.astype(jnp.bfloat16)
    w_high[...] = high
    w_low[...] = (weights - high.astype(jnp.float32)).astype(jnp.bfloat16)
    for shift, out in ((1, next_ref), (2, across_ref), (3, previous_ref)):
        rows = pl.ds(pl.multiple_of(lax.rem(me_ref[0] + shift, 4) * 64, 64), 64)
        skip = high_ref.shape[1] - out.shape[2]
        value = product(w_high[rows, :], w_low[rows, :], high_ref[:, skip:], low_ref[:, skip:])
        out[...] = value.reshape(out.shape)


def factorise(me, terms, high, low, scale):
    columns = high.shape[-1]
    return pl.pallas_call(
        lambda *refs: factor_kernel(scale, *refs),
        in_specs=[SMEM] + [FULL] * 3,
        out_specs=[FULL] * 6,
        out_shape=[jax.ShapeDtypeStruct((1, NV), jnp.float32)]
        + [jax.ShapeDtypeStruct((8 * NV, 8 * NV), jnp.bfloat16)] * 2
        + [
            jax.ShapeDtypeStruct((8, 8, width), jnp.float32)
            for width in (columns, columns - NEAR, columns)
        ],
        compiler_params=params(),
    )(me, terms, high, low)


def product(w_high, w_low, high, low):
    value = jnp.dot(w_high, high, preferred_element_type=jnp.float32)
    value += jnp.dot(w_high, low, preferred_element_type=jnp.float32)
    return value + jnp.dot(w_low, high, preferred_element_type=jnp.float32)


def own_kernel(me_ref, w_high, w_low, high_ref, low_ref, *refs):
    pieces, (out, own_ref, far_ref, far_high, far_low, sems) = refs[:-6], refs[-6:]
    me = me_ref[0]
    for back, piece in enumerate(pieces):
        start = pl.multiple_of(lax.rem(me + 4 - back, 4) * 64, 64)
        high, low = split(piece[...].reshape(64, piece.shape[2]))
        far_high[pl.ds(start, 64), :] = high
        far_low[pl.ds(start, 64), :] = low
    rows = pl.ds(pl.multiple_of(me * 64, 64), 64)
    own_high, own_low = w_high[rows, :], w_low[rows, :]
    own_ref[...] = product(own_high, own_low, high_ref[...], low_ref[...]).reshape(own_ref.shape)
    own_copy = pltpu.make_async_copy(own_ref, out.at[:, me], sems.at[0])
    own_copy.start()
    far_ref[...] = product(own_high, own_low, far_high[...], far_low[...]).reshape(far_ref.shape)
    far_copy = pltpu.make_async_copy(
        far_ref, out.at[:, lax.rem(me + 2, 4), :, pl.ds(0, NEAR)], sems.at[1]
    )
    far_copy.start()
    own_copy.wait()
    far_copy.wait()


def own_parts(me, w_high, w_low, high, low, pieces):
    columns = high.shape[-1]
    return pl.pallas_call(
        own_kernel,
        in_specs=[SMEM] + [FULL] * (4 + len(pieces)),
        out_specs=HBM,
        out_shape=jax.ShapeDtypeStruct((8, 4, 8, columns), jnp.float32),
        scratch_shapes=[
            pltpu.VMEM((8, 8, columns), jnp.float32),
            pltpu.VMEM((8, 8, NEAR), jnp.float32),
            pltpu.VMEM((8 * NV, NEAR), jnp.bfloat16),
            pltpu.VMEM((8 * NV, NEAR), jnp.bfloat16),
            pltpu.SemaphoreType.DMA((2,)),
        ],
        compiler_params=params(),
    )(me, w_high, w_low, high, low, *pieces)


def assemble_kernel(me_ref, own_ref, before_ref, across_ref, after_ref, out, sems):
    me = me_ref[0]
    width = across_ref.shape[2]
    far = out.at[:, lax.rem(me + 2, 4), :, pl.ds(out.shape[3] - width, width)]
    copies = [
        pltpu.make_async_copy(before_ref, out.at[:, lax.rem(me + 3, 4)], sems.at[0]),
        pltpu.make_async_copy(after_ref, out.at[:, lax.rem(me + 1, 4)], sems.at[1]),
        pltpu.make_async_copy(across_ref, far, sems.at[2]),
    ]
    for copy in copies:
        copy.start()
    for copy in copies:
        copy.wait()


def assemble(me, own, before, across, after):
    return pl.pallas_call(
        assemble_kernel,
        in_specs=[SMEM, HBM] + [pl.BlockSpec(memory_space=pl.ANY)] * 3,
        out_specs=HBM,
        out_shape=jax.ShapeDtypeStruct(own.shape, own.dtype),
        scratch_shapes=[pltpu.SemaphoreType.DMA((3,))],
        input_output_aliases={1: 0},
        compiler_params=params(),
    )(me, own, before, across, after)


def shifted(block, shift):
    return lax.ppermute(block, "vec", [(i, (i + shift) % 4) for i in range(4)])


def exchange(blocks):
    moved = {shift: shifted(blocks[shift], shift) for shift in (2, 1, 3)}
    return [blocks[0], moved[1], moved[2], moved[3]]


def opposite(blocks):
    one = lax.ppermute(blocks[3], "vec", [(0, 1), (1, 2), (2, 3)])
    two = lax.ppermute(blocks[0], "vec", [(0, 2), (1, 3)])
    three = lax.ppermute(blocks[1], "vec", [(0, 3)])
    return [blocks[2], one, two, three]


def all_terms(copies):
    return lax.all_to_all(copies, ("rows", "vec"), 0, 0, tiled=True)


CHUNKS = (2, 6)
NEAR = 2048


def per_device(lattice_state, constant_field, tangents):
    me = lax.axis_index("vec").astype(jnp.int32).reshape(1)
    rows, columns = lattice_state.shape[1:]
    scale = math.sqrt(2.0 * rows * lax.axis_size("rows") * columns)
    sources = (lattice_state[None], constant_field[None], tangents[: CHUNKS[0]])
    ahead = neighbours(
        *(jnp.concatenate(parts, axis=0) for parts in zip(*(edges(part) for part in sources)))
    )
    ahead, rest = lax.optimization_barrier((ahead, edges(tangents[CHUNKS[0] :])))
    halos = [ahead, neighbours(*rest)]
    pieces, local, start = [], [], 0
    for count, halo in zip(CHUNKS, halos):
        if pieces:
            halo, blocks = lax.optimization_barrier((halo, blocks))
            blocks = push(me, tangents, halo, twice, start, count)
        else:
            blocks, twice, next_state = push_first(
                me, lattice_state, constant_field, tangents, halo, count
            )
        if pieces:
            blocks, pieces = lax.optimization_barrier((blocks, pieces))
        local.append(blocks)
        pieces += exchange(blocks)
        start += count
    slabs = [
        jnp.concatenate([blocks[shift][:, :, :NEAR] for blocks in local], axis=0)
        for shift in range(4)
    ]
    slabs, pieces[5] = lax.optimization_barrier((slabs, pieces[5]))
    far = opposite(slabs)
    high, low, copies = inner_products(me, pieces, len(CHUNKS))
    terms, far = lax.optimization_barrier((all_terms(copies), far))
    growth, w_high, w_low, following, across, previous = factorise(me, terms, high, low, scale)
    across = shifted(across, 2)
    before = shifted(following, 1)
    after = shifted(previous, 3)
    own = own_parts(me, w_high, w_low, high, low, far)
    basis = assemble(me, own, before, across, after)
    return (next_state, basis.reshape(tangents.shape), growth.reshape(NV))


def solution(mesh):
    return jax.shard_map(
        per_device,
        mesh=mesh,
        in_specs=(P(None, "rows", None), P(None, "rows", None), P("vec", None, "rows", None)),
        out_specs=(P(None, "rows", None), P("vec", None, "rows", None), P()),
        check_vma=False,
    )
```

```python
import math

import jax
import jax.numpy as jnp
from jax import lax
from jax.experimental import pallas as pl
from jax.experimental.pallas import tpu as pltpu
from jax.sharding import PartitionSpec as P

NV = 32
STEPS = 3
COUPLING = 0.35
HALO = 4
VMEM = 24 * 1024 * 1024
HIGHEST = lax.Precision.HIGHEST
FULL = pl.BlockSpec(memory_space=pltpu.VMEM)
SMEM = pl.BlockSpec(memory_space=pltpu.SMEM)
HBM = pl.BlockSpec(memory_space=pltpu.HBM)


def params():
    return pltpu.CompilerParams(vmem_limit_bytes=VMEM)


def edges(block):
    last = lax.slice_in_dim(block, block.shape[2] - HALO, None, axis=2)
    return last, lax.slice_in_dim(block, 0, HALO, axis=2)


def neighbours(last, first):
    count = lax.axis_size("rows")
    forward = [(i, (i + 1) % count) for i in range(count)]
    backward = [(target, source) for source, target in forward]
    above = lax.ppermute(last, "rows", forward)
    below = lax.ppermute(first, "rows", backward)
    return below, above


def mix(field):
    rows, columns = field.shape
    beside = (
        pltpu.roll(field, 1, 0)
        + pltpu.roll(field, rows - 1, 0)
        + pltpu.roll(field, 1, 1)
        + pltpu.roll(field, columns - 1, 1)
    )
    return (1.0 - COUPLING) * field + (COUPLING / 4.0) * beside


def ring(block, below, above):
    return jnp.concatenate([block, below, above], axis=0)


def lattice_kernel(z_ref, c_ref, below_ref, above_ref, twice_ref, next_ref):
    real, imag = (ring(z_ref[i], below_ref[0, i], above_ref[0, i]) for i in range(2))
    const_real, const_imag = (ring(c_ref[i], below_ref[1, i], above_ref[1, i]) for i in range(2))
    for step in range(STEPS):
        twice_ref[step, 0] = 2.0 * real
        twice_ref[step, 1] = 2.0 * imag
        map_real = real * real - imag * imag + const_real
        map_imag = 2.0 * real * imag + const_imag
        real, imag = mix(map_real), mix(map_imag)
    rows = z_ref.shape[1]
    next_ref[0] = real[:rows]
    next_ref[1] = imag[:rows]


def tangent_kernel(me_ref, u_ref, below_ref, above_ref, twice_ref, *rest):
    outs, slabs = rest[:-1], rest[-1]
    real, imag = (ring(u_ref[0, i], below_ref[0, i], above_ref[0, i]) for i in range(2))
    for step in range(STEPS):
        z_real, z_imag = twice_ref[step, 0], twice_ref[step, 1]
        push_real = z_real * real - z_imag * imag
        push_imag = z_real * imag + z_imag * real
        real, imag = mix(push_real), mix(push_imag)
    slabs[0] = real[:8]
    slabs[1] = real[8:16]
    slabs[2] = imag[:8]
    slabs[3] = imag[8:16]
    for shift, out in enumerate(outs):
        out[0] = slabs[lax.rem(me_ref[0] + shift, 4)]


def first_kernel(
    me_ref,
    u_ref,
    below_ref,
    above_ref,
    z_ref,
    c_ref,
    fields_below,
    fields_above,
    *rest,
):
    outs, twice_ref, next_ref, slabs = rest[:-3], *rest[-3:]

    @pl.when(pl.program_id(0) == 0)
    def _():
        lattice_kernel(z_ref, c_ref, fields_below, fields_above, twice_ref, next_ref)

    tangent_kernel(me_ref, u_ref, below_ref, above_ref, twice_ref, *outs, slabs)


def push_first(me, lattice_state, constant_field, vectors, halo, count):
    rows, columns = lattice_state.shape[1:]
    edge = pl.BlockSpec((1, 2, HALO, columns), lambda i: (2 + i, 0, 0, 0))
    fields = pl.BlockSpec((2, 2, HALO, columns), lambda i: (0, 0, 0, 0))
    *blocks, twice, next_state = pl.pallas_call(
        first_kernel,
        grid=(count,),
        in_specs=[
            SMEM,
            pl.BlockSpec((1, 2, rows, columns), lambda i: (i, 0, 0, 0)),
            edge,
            edge,
            FULL,
            FULL,
            fields,
            fields,
        ],
        out_specs=[pl.BlockSpec((1, 8, columns), lambda i: (i, 0, 0))] * 4 + [FULL] * 2,
        out_shape=[jax.ShapeDtypeStruct((count, 8, columns), jnp.float32)] * 4
        + [
            jax.ShapeDtypeStruct((STEPS, 2, rows + 2 * HALO, columns), jnp.float32),
            jax.ShapeDtypeStruct((2, rows, columns), jnp.float32),
        ],
        scratch_shapes=[pltpu.VMEM((4, 8, columns), jnp.float32)],
        compiler_params=params(),
        cost_estimate=pl.CostEstimate(
            flops=count * 45_000_000, bytes_accessed=count * 9_000_000, transcendentals=0
        ),
    )(
        me,
        pltpu.with_memory_space_constraint(vectors, pltpu.HBM),
        *halo,
        lattice_state,
        constant_field,
        *halo,
    )
    return blocks, twice, next_state


def push(me, vectors, halo, twice, start, count):
    columns = vectors.shape[-1]
    skip = halo[0].shape[0] - count
    return pl.pallas_call(
        tangent_kernel,
        grid=(count,),
        in_specs=[
            SMEM,
            pl.BlockSpec((1, 2, 16, columns), lambda i: (start + i, 0, 0, 0)),
            pl.BlockSpec((1, 2, HALO, columns), lambda i: (skip + i, 0, 0, 0)),
            pl.BlockSpec((1, 2, HALO, columns), lambda i: (skip + i, 0, 0, 0)),
            FULL,
        ],
        out_specs=[pl.BlockSpec((1, 8, columns), lambda i: (i, 0, 0))] * 4,
        out_shape=[jax.ShapeDtypeStruct((count, 8, columns), jnp.float32)] * 4,
        scratch_shapes=[pltpu.VMEM((4, 8, columns), jnp.float32)],
        compiler_params=params(),
        cost_estimate=pl.CostEstimate(
            flops=count * 30_000_000, bytes_accessed=count * 6_000_000, transcendentals=0
        ),
    )(me, pltpu.with_memory_space_constraint(vectors, pltpu.HBM), *halo, twice)


def same_row(shape, period):
    return lax.rem(lax.broadcasted_iota(jnp.int32, shape, 0), period) == lax.rem(
        lax.broadcasted_iota(jnp.int32, shape, 1), period
    )


def owner(shape, group):
    row = lax.broadcasted_iota(jnp.int32, shape, 0)
    column = lax.broadcasted_iota(jnp.int32, shape, 1)
    return jnp.where(row == lax.div(column, group), 1.0, 0.0)


def split(value):
    high = value.astype(jnp.bfloat16)
    return high, (value - high.astype(jnp.float32)).astype(jnp.bfloat16)


def gram_kernel(chunks, me_ref, *refs):
    pieces = refs[: 4 * chunks]
    high_ref, low_ref, gram_ref = refs[4 * chunks :]
    offset = 0
    for chunk in range(chunks):
        count, rows, columns = pieces[4 * chunk].shape
        for shift in range(4):
            source = lax.rem(me_ref[0] + 4 - shift, 4)
            start = pl.multiple_of(source * 64 + offset, 16)
            high, low = split(pieces[4 * chunk + shift][...].reshape(count * rows, columns))
            high_ref[pl.ds(start, count * rows), :] = high
            low_ref[pl.ds(start, count * rows), :] = low
        offset += count * rows
    high = high_ref[...]
    low = low_ref[...]
    last = (((1,), (1,)), ((), ()))
    main = lax.dot_general(high, high, last, preferred_element_type=jnp.float32)
    rest = lax.dot_general(high, low, last, preferred_element_type=jnp.float32)
    full = main + (rest + rest.T)
    full = jnp.where(same_row(full.shape, 8), full, 0.0)
    left = full.reshape(NV, 8, 8 * NV).sum(1)
    gram = lax.dot_general(
        left, owner((NV, 8 * NV), 8), last, precision=HIGHEST, preferred_element_type=jnp.float32
    )
    packed = jnp.concatenate([gram[8 * i : 8 * i + 8] for i in range(4)], axis=1)
    copies = gram_ref.shape[0] // 8
    gram_ref[...] = jnp.broadcast_to(packed[None], (copies, 8, 4 * NV)).reshape(gram_ref.shape)


def inner_products(me, pieces, chunks):
    columns = pieces[0].shape[-1]
    devices = lax.axis_size("rows") * lax.axis_size("vec")
    return pl.pallas_call(
        lambda *refs: gram_kernel(chunks, *refs),
        in_specs=[SMEM] + [FULL] * len(pieces),
        out_specs=[FULL] * 3,
        out_shape=[
            jax.ShapeDtypeStruct((8 * NV, columns), jnp.bfloat16),
            jax.ShapeDtypeStruct((8 * NV, columns), jnp.bfloat16),
            jax.ShapeDtypeStruct((8 * devices, 4 * NV), jnp.float32),
        ],
        compiler_params=params(),
    )(me, *pieces)


def factor_kernel(
    scale,
    me_ref,
    terms_ref,
    high_ref,
    low_ref,
    growth_ref,
    w_high,
    w_low,
    next_ref,
    across_ref,
    previous_ref,
):
    row = lax.broadcasted_iota(jnp.int32, (NV, 2 * NV), 0)
    column = lax.broadcasted_iota(jnp.int32, (NV, 2 * NV), 1)
    spread = jnp.where(row == column, 1.0, 0.0)
    last = (((1,), (0,)), ((), ()))
    packed = jnp.sum(terms_ref[...].reshape(terms_ref.shape[0] // 8, 8, 4 * NV), axis=0)
    gram = jnp.concatenate([packed[:, NV * i : NV * i + NV] for i in range(4)], axis=0)
    work = jnp.where(column == row + NV, 1.0, 0.0) + lax.dot_general(
        gram, spread, last, precision=HIGHEST, preferred_element_type=jnp.float32
    )
    for k in range(NV):
        pivot_row = work[k : k + 1, :]
        pivot = pivot_row[:, k : k + 1]
        inverse = lax.rsqrt(pivot)
        inverse = inverse * (1.5 - 0.5 * pivot * inverse * inverse)
        scaled = pivot_row * inverse
        factor = work[:, k : k + 1] * inverse
        work = jnp.where(row > k, work - factor * scaled, jnp.where(row == k, scaled, work))
    diagonal = jnp.sum(jnp.where(column == row, work, 0.0), axis=0, keepdims=True)
    growth_ref[...] = jnp.log(diagonal[:, :NV] / scale)
    inverse = work[:, NV:] * scale
    wide = lax.dot_general(
        inverse,
        owner((NV, 8 * NV), 8),
        last,
        precision=HIGHEST,
        preferred_element_type=jnp.float32,
    )
    tall = jnp.broadcast_to(wide[:, None, :], (NV, 8, 8 * NV)).reshape(8 * NV, 8 * NV)
    weights = jnp.where(same_row(tall.shape, 8), tall, 0.0)
    high = weights.astype(jnp.bfloat16)
    w_high[...] = high
    w_low[...] = (weights - high.astype(jnp.float32)).astype(jnp.bfloat16)
    for shift, out in ((1, next_ref), (2, across_ref), (3, previous_ref)):
        rows = pl.ds(pl.multiple_of(lax.rem(me_ref[0] + shift, 4) * 64, 64), 64)
        skip = high_ref.shape[1] - out.shape[2]
        value = product(w_high[rows, :], w_low[rows, :], high_ref[:, skip:], low_ref[:, skip:])
        out[...] = value.reshape(out.shape)


def factorise(me, terms, high, low, scale):
    columns = high.shape[-1]
    return pl.pallas_call(
        lambda *refs: factor_kernel(scale, *refs),
        in_specs=[SMEM] + [FULL] * 3,
        out_specs=[FULL] * 6,
        out_shape=[jax.ShapeDtypeStruct((1, NV), jnp.float32)]
        + [jax.ShapeDtypeStruct((8 * NV, 8 * NV), jnp.bfloat16)] * 2
        + [
            jax.ShapeDtypeStruct((8, 8, width), jnp.float32)
            for width in (columns, columns - NEAR, columns)
        ],
        compiler_params=params(),
    )(me, terms, high, low)


def product(w_high, w_low, high, low):
    value = jnp.dot(w_high, high, preferred_element_type=jnp.float32)
    value += jnp.dot(w_high, low, preferred_element_type=jnp.float32)
    return value + jnp.dot(w_low, high, preferred_element_type=jnp.float32)


def own_kernel(me_ref, w_high, w_low, high_ref, low_ref, *refs):
    pieces, (out, own_ref, far_ref, far_high, far_low, sems) = refs[:-6], refs[-6:]
    me = me_ref[0]
    for back, piece in enumerate(pieces):
        start = pl.multiple_of(lax.rem(me + 4 - back, 4) * 64, 64)
        high, low = split(piece[...].reshape(64, piece.shape[2]))
        far_high[pl.ds(start, 64), :] = high
        far_low[pl.ds(start, 64), :] = low
    rows = pl.ds(pl.multiple_of(me * 64, 64), 64)
    own_high, own_low = w_high[rows, :], w_low[rows, :]
    own_ref[...] = product(own_high, own_low, high_ref[...], low_ref[...]).reshape(own_ref.shape)
    own_copy = pltpu.make_async_copy(own_ref, out.at[:, me], sems.at[0])
    own_copy.start()
    far_ref[...] = product(own_high, own_low, far_high[...], far_low[...]).reshape(far_ref.shape)
    far_copy = pltpu.make_async_copy(
        far_ref, out.at[:, lax.rem(me + 2, 4), :, pl.ds(0, NEAR)], sems.at[1]
    )
    far_copy.start()
    own_copy.wait()
    far_copy.wait()


def own_parts(me, w_high, w_low, high, low, pieces):
    columns = high.shape[-1]
    return pl.pallas_call(
        own_kernel,
        in_specs=[SMEM] + [FULL] * (4 + len(pieces)),
        out_specs=HBM,
        out_shape=jax.ShapeDtypeStruct((8, 4, 8, columns), jnp.float32),
        scratch_shapes=[
            pltpu.VMEM((8, 8, columns), jnp.float32),
            pltpu.VMEM((8, 8, NEAR), jnp.float32),
            pltpu.VMEM((8 * NV, NEAR), jnp.bfloat16),
            pltpu.VMEM((8 * NV, NEAR), jnp.bfloat16),
            pltpu.SemaphoreType.DMA((2,)),
        ],
        compiler_params=params(),
    )(me, w_high, w_low, high, low, *pieces)


def assemble_kernel(me_ref, own_ref, before_ref, across_ref, after_ref, out, sems):
    me = me_ref[0]
    width = across_ref.shape[2]
    far = out.at[:, lax.rem(me + 2, 4), :, pl.ds(out.shape[3] - width, width)]
    copies = [
        pltpu.make_async_copy(before_ref, out.at[:, lax.rem(me + 3, 4)], sems.at[0]),
        pltpu.make_async_copy(after_ref, out.at[:, lax.rem(me + 1, 4)], sems.at[1]),
        pltpu.make_async_copy(across_ref, far, sems.at[2]),
    ]
    for copy in copies:
        copy.start()
    for copy in copies:
        copy.wait()


def assemble(me, own, before, across, after):
    return pl.pallas_call(
        assemble_kernel,
        in_specs=[SMEM, HBM] + [pl.BlockSpec(memory_space=pl.ANY)] * 3,
        out_specs=HBM,
        out_shape=jax.ShapeDtypeStruct(own.shape, own.dtype),
        scratch_shapes=[pltpu.SemaphoreType.DMA((3,))],
        input_output_aliases={1: 0},
        compiler_params=params(),
    )(me, own, before, across, after)


def shifted(block, shift):
    return lax.ppermute(block, "vec", [(i, (i + shift) % 4) for i in range(4)])


def exchange(blocks):
    moved = {shift: shifted(blocks[shift], shift) for shift in (2, 1, 3)}
    return [blocks[0], moved[1], moved[2], moved[3]]


def opposite(blocks):
    one = lax.ppermute(blocks[3], "vec", [(0, 1), (1, 2), (2, 3)])
    two = lax.ppermute(blocks[0], "vec", [(0, 2), (1, 3)])
    three = lax.ppermute(blocks[1], "vec", [(0, 3)])
    return [blocks[2], one, two, three]


def all_terms(copies):
    return lax.all_to_all(copies, ("rows", "vec"), 0, 0, tiled=True)


CHUNKS = (2, 6)
NEAR = 2304


def per_device(lattice_state, constant_field, tangents):
    me = lax.axis_index("vec").astype(jnp.int32).reshape(1)
    rows, columns = lattice_state.shape[1:]
    scale = math.sqrt(2.0 * rows * lax.axis_size("rows") * columns)
    sources = (lattice_state[None], constant_field[None], tangents[: CHUNKS[0]])
    ahead = neighbours(
        *(jnp.concatenate(parts, axis=0) for parts in zip(*(edges(part) for part in sources)))
    )
    ahead, rest = lax.optimization_barrier((ahead, edges(tangents[CHUNKS[0] :])))
    halos = [ahead, neighbours(*rest)]
    pieces, local, start = [], [], 0
    for count, halo in zip(CHUNKS, halos):
        if pieces:
            halo, blocks = lax.optimization_barrier((halo, blocks))
            blocks = push(me, tangents, halo, twice, start, count)
        else:
            blocks, twice, next_state = push_first(
                me, lattice_state, constant_field, tangents, halo, count
            )
        if pieces:
            blocks, pieces = lax.optimization_barrier((blocks, pieces))
        local.append(blocks)
        pieces += exchange(blocks)
        start += count
    slabs = [
        jnp.concatenate([blocks[shift][:, :, :NEAR] for blocks in local], axis=0)
        for shift in range(4)
    ]
    slabs, pieces[5] = lax.optimization_barrier((slabs, pieces[5]))
    far = opposite(slabs)
    high, low, copies = inner_products(me, pieces, len(CHUNKS))
    terms, far = lax.optimization_barrier((all_terms(copies), far))
    growth, w_high, w_low, following, across, previous = factorise(me, terms, high, low, scale)
    across = shifted(across, 2)
    before = shifted(following, 1)
    after = shifted(previous, 3)
    own = own_parts(me, w_high, w_low, high, low, far)
    basis = assemble(me, own, before, across, after)
    return (next_state, basis.reshape(tangents.shape), growth.reshape(NV))


def solution(mesh):
    return jax.shard_map(
        per_device,
        mesh=mesh,
        in_specs=(P(None, "rows", None), P(None, "rows", None), P("vec", None, "rows", None)),
        out_specs=(P(None, "rows", None), P("vec", None, "rows", None), P()),
        check_vma=False,
    )
```

```python
import math

import jax
import jax.numpy as jnp
from jax import lax
from jax.experimental import pallas as pl
from jax.experimental.pallas import tpu as pltpu
from jax.sharding import PartitionSpec as P

NV = 32
STEPS = 3
COUPLING = 0.35
HALO = 4
VMEM = 32 * 1024 * 1024
HIGHEST = lax.Precision.HIGHEST
FULL = pl.BlockSpec(memory_space=pltpu.VMEM)
SMEM = pl.BlockSpec(memory_space=pltpu.SMEM)
HBM = pl.BlockSpec(memory_space=pltpu.HBM)


def params():
    return pltpu.CompilerParams(vmem_limit_bytes=VMEM)


def edges(block):
    last = lax.slice_in_dim(block, block.shape[2] - HALO, None, axis=2)
    return last, lax.slice_in_dim(block, 0, HALO, axis=2)


def neighbours(last, first):
    count = lax.axis_size("rows")
    forward = [(i, (i + 1) % count) for i in range(count)]
    backward = [(target, source) for source, target in forward]
    above = lax.ppermute(last, "rows", forward)
    below = lax.ppermute(first, "rows", backward)
    return below, above


def mix(field):
    rows, columns = field.shape
    beside = (
        pltpu.roll(field, 1, 0)
        + pltpu.roll(field, rows - 1, 0)
        + pltpu.roll(field, 1, 1)
        + pltpu.roll(field, columns - 1, 1)
    )
    return (1.0 - COUPLING) * field + (COUPLING / 4.0) * beside


def ring(block, below, above):
    return jnp.concatenate([block, below, above], axis=0)


def lattice_kernel(z_ref, c_ref, below_ref, above_ref, twice_ref, next_ref):
    real, imag = (ring(z_ref[i], below_ref[0, i], above_ref[0, i]) for i in range(2))
    const_real, const_imag = (ring(c_ref[i], below_ref[1, i], above_ref[1, i]) for i in range(2))
    for step in range(STEPS):
        twice_ref[step, 0] = 2.0 * real
        twice_ref[step, 1] = 2.0 * imag
        map_real = real * real - imag * imag + const_real
        map_imag = 2.0 * real * imag + const_imag
        real, imag = mix(map_real), mix(map_imag)
    rows = z_ref.shape[1]
    next_ref[0] = real[:rows]
    next_ref[1] = imag[:rows]


def tangent_kernel(me_ref, u_ref, below_ref, above_ref, twice_ref, *rest):
    outs, slabs = rest[:-1], rest[-1]
    real, imag = (ring(u_ref[0, i], below_ref[0, i], above_ref[0, i]) for i in range(2))
    for step in range(STEPS):
        z_real, z_imag = twice_ref[step, 0], twice_ref[step, 1]
        push_real = z_real * real - z_imag * imag
        push_imag = z_real * imag + z_imag * real
        real, imag = mix(push_real), mix(push_imag)
    slabs[0] = real[:8]
    slabs[1] = real[8:16]
    slabs[2] = imag[:8]
    slabs[3] = imag[8:16]
    for shift, out in enumerate(outs):
        out[0] = slabs[lax.rem(me_ref[0] + shift, 4)]


def first_kernel(
    me_ref,
    u_ref,
    below_ref,
    above_ref,
    z_ref,
    c_ref,
    fields_below,
    fields_above,
    *rest,
):
    outs, twice_ref, next_ref, slabs = rest[:-3], *rest[-3:]

    @pl.when(pl.program_id(0) == 0)
    def _():
        lattice_kernel(z_ref, c_ref, fields_below, fields_above, twice_ref, next_ref)

    tangent_kernel(me_ref, u_ref, below_ref, above_ref, twice_ref, *outs, slabs)


def push_first(me, lattice_state, constant_field, vectors, halo, count):
    rows, columns = lattice_state.shape[1:]
    edge = pl.BlockSpec((1, 2, HALO, columns), lambda i: (2 + i, 0, 0, 0))
    fields = pl.BlockSpec((2, 2, HALO, columns), lambda i: (0, 0, 0, 0))
    *blocks, twice, next_state = pl.pallas_call(
        first_kernel,
        grid=(count,),
        in_specs=[
            SMEM,
            pl.BlockSpec((1, 2, rows, columns), lambda i: (i, 0, 0, 0)),
            edge,
            edge,
            FULL,
            FULL,
            fields,
            fields,
        ],
        out_specs=[pl.BlockSpec((1, 8, columns), lambda i: (i, 0, 0))] * 4 + [FULL] * 2,
        out_shape=[jax.ShapeDtypeStruct((count, 8, columns), jnp.float32)] * 4
        + [
            jax.ShapeDtypeStruct((STEPS, 2, rows + 2 * HALO, columns), jnp.float32),
            jax.ShapeDtypeStruct((2, rows, columns), jnp.float32),
        ],
        scratch_shapes=[pltpu.VMEM((4, 8, columns), jnp.float32)],
        compiler_params=params(),
        cost_estimate=pl.CostEstimate(
            flops=count * 45_000_000, bytes_accessed=count * 9_000_000, transcendentals=0
        ),
    )(
        me,
        pltpu.with_memory_space_constraint(vectors, pltpu.HBM),
        *halo,
        lattice_state,
        constant_field,
        *halo,
    )
    return blocks, twice, next_state


def push(me, vectors, halo, twice, start, count):
    columns = vectors.shape[-1]
    skip = halo[0].shape[0] - count
    return pl.pallas_call(
        tangent_kernel,
        grid=(count,),
        in_specs=[
            SMEM,
            pl.BlockSpec((1, 2, 16, columns), lambda i: (start + i, 0, 0, 0)),
            pl.BlockSpec((1, 2, HALO, columns), lambda i: (skip + i, 0, 0, 0)),
            pl.BlockSpec((1, 2, HALO, columns), lambda i: (skip + i, 0, 0, 0)),
            FULL,
        ],
        out_specs=[pl.BlockSpec((1, 8, columns), lambda i: (i, 0, 0))] * 4,
        out_shape=[jax.ShapeDtypeStruct((count, 8, columns), jnp.float32)] * 4,
        scratch_shapes=[pltpu.VMEM((4, 8, columns), jnp.float32)],
        compiler_params=params(),
        cost_estimate=pl.CostEstimate(
            flops=count * 30_000_000, bytes_accessed=count * 6_000_000, transcendentals=0
        ),
    )(me, pltpu.with_memory_space_constraint(vectors, pltpu.HBM), *halo, twice)


def same_row(shape, period):
    return lax.rem(lax.broadcasted_iota(jnp.int32, shape, 0), period) == lax.rem(
        lax.broadcasted_iota(jnp.int32, shape, 1), period
    )


def owner(shape, group):
    row = lax.broadcasted_iota(jnp.int32, shape, 0)
    column = lax.broadcasted_iota(jnp.int32, shape, 1)
    return jnp.where(row == lax.div(column, group), 1.0, 0.0)


def split(value):
    high = value.astype(jnp.bfloat16)
    return high, (value - high.astype(jnp.float32)).astype(jnp.bfloat16)


def gram_kernel(chunks, me_ref, *refs):
    pieces = refs[: 4 * chunks]
    high_ref, low_ref, gram_ref = refs[4 * chunks :]
    offset = 0
    for chunk in range(chunks):
        count, rows, columns = pieces[4 * chunk].shape
        for shift in range(4):
            source = lax.rem(me_ref[0] + 4 - shift, 4)
            start = pl.multiple_of(source * 64 + offset, 16)
            high, low = split(pieces[4 * chunk + shift][...].reshape(count * rows, columns))
            high_ref[pl.ds(start, count * rows), :] = high
            low_ref[pl.ds(start, count * rows), :] = low
        offset += count * rows
    high = high_ref[...]
    low = low_ref[...]
    last = (((1,), (1,)), ((), ()))
    main = lax.dot_general(high, high, last, preferred_element_type=jnp.float32)
    rest = lax.dot_general(high, low, last, preferred_element_type=jnp.float32)
    full = main + (rest + rest.T)
    full = jnp.where(same_row(full.shape, 8), full, 0.0)
    left = full.reshape(NV, 8, 8 * NV).sum(1)
    gram = lax.dot_general(
        left, owner((NV, 8 * NV), 8), last, precision=HIGHEST, preferred_element_type=jnp.float32
    )
    packed = jnp.concatenate([gram[8 * i : 8 * i + 8] for i in range(4)], axis=1)
    copies = gram_ref.shape[0] // 8
    gram_ref[...] = jnp.broadcast_to(packed[None], (copies, 8, 4 * NV)).reshape(gram_ref.shape)


def inner_products(me, pieces, chunks):
    columns = pieces[0].shape[-1]
    devices = lax.axis_size("rows") * lax.axis_size("vec")
    return pl.pallas_call(
        lambda *refs: gram_kernel(chunks, *refs),
        in_specs=[SMEM] + [FULL] * len(pieces),
        out_specs=[FULL] * 3,
        out_shape=[
            jax.ShapeDtypeStruct((8 * NV, columns), jnp.bfloat16),
            jax.ShapeDtypeStruct((8 * NV, columns), jnp.bfloat16),
            jax.ShapeDtypeStruct((8 * devices, 4 * NV), jnp.float32),
        ],
        compiler_params=params(),
    )(me, *pieces)


def factor_kernel(
    scale,
    me_ref,
    terms_ref,
    high_ref,
    low_ref,
    growth_ref,
    w_high,
    w_low,
    next_ref,
    across_ref,
    previous_ref,
):
    row = lax.broadcasted_iota(jnp.int32, (NV, 2 * NV), 0)
    column = lax.broadcasted_iota(jnp.int32, (NV, 2 * NV), 1)
    spread = jnp.where(row == column, 1.0, 0.0)
    last = (((1,), (0,)), ((), ()))
    packed = jnp.sum(terms_ref[...].reshape(terms_ref.shape[0] // 8, 8, 4 * NV), axis=0)
    gram = jnp.concatenate([packed[:, NV * i : NV * i + NV] for i in range(4)], axis=0)
    work = jnp.where(column == row + NV, 1.0, 0.0) + lax.dot_general(
        gram, spread, last, precision=HIGHEST, preferred_element_type=jnp.float32
    )
    for k in range(NV):
        pivot_row = work[k : k + 1, :]
        pivot = pivot_row[:, k : k + 1]
        inverse = lax.rsqrt(pivot)
        inverse = inverse * (1.5 - 0.5 * pivot * inverse * inverse)
        scaled = pivot_row * inverse
        factor = work[:, k : k + 1] * inverse
        work = jnp.where(row > k, work - factor * scaled, jnp.where(row == k, scaled, work))
    diagonal = jnp.sum(jnp.where(column == row, work, 0.0), axis=0, keepdims=True)
    growth_ref[...] = jnp.log(diagonal[:, :NV] / scale)
    inverse = work[:, NV:] * scale
    wide = lax.dot_general(
        inverse,
        owner((NV, 8 * NV), 8),
        last,
        precision=HIGHEST,
        preferred_element_type=jnp.float32,
    )
    tall = jnp.broadcast_to(wide[:, None, :], (NV, 8, 8 * NV)).reshape(8 * NV, 8 * NV)
    weights = jnp.where(same_row(tall.shape, 8), tall, 0.0)
    high = weights.astype(jnp.bfloat16)
    w_high[...] = high
    w_low[...] = (weights - high.astype(jnp.float32)).astype(jnp.bfloat16)
    for shift, out in ((1, next_ref), (2, across_ref), (3, previous_ref)):
        rows = pl.ds(pl.multiple_of(lax.rem(me_ref[0] + shift, 4) * 64, 64), 64)
        skip = high_ref.shape[1] - out.shape[2]
        value = product(w_high[rows, :], w_low[rows, :], high_ref[:, skip:], low_ref[:, skip:])
        out[...] = value.reshape(out.shape)


def factorise(me, terms, high, low, scale):
    columns = high.shape[-1]
    return pl.pallas_call(
        lambda *refs: factor_kernel(scale, *refs),
        in_specs=[SMEM] + [FULL] * 3,
        out_specs=[FULL] * 6,
        out_shape=[jax.ShapeDtypeStruct((1, NV), jnp.float32)]
        + [jax.ShapeDtypeStruct((8 * NV, 8 * NV), jnp.bfloat16)] * 2
        + [
            jax.ShapeDtypeStruct((8, 8, width), jnp.float32)
            for width in (columns, columns - NEAR, columns)
        ],
        compiler_params=params(),
    )(me, terms, high, low)


def product(w_high, w_low, high, low):
    value = jnp.dot(w_high, high, preferred_element_type=jnp.float32)
    value += jnp.dot(w_high, low, preferred_element_type=jnp.float32)
    return value + jnp.dot(w_low, high, preferred_element_type=jnp.float32)


def own_kernel(me_ref, w_high, w_low, high_ref, low_ref, *refs):
    pieces, (out, own_ref, far_ref, far_high, far_low, sems) = refs[:-6], refs[-6:]
    me = me_ref[0]
    for back, piece in enumerate(pieces):
        start = pl.multiple_of(lax.rem(me + 4 - back, 4) * 64, 64)
        high, low = split(piece[...].reshape(64, piece.shape[2]))
        far_high[pl.ds(start, 64), :] = high
        far_low[pl.ds(start, 64), :] = low
    rows = pl.ds(pl.multiple_of(me * 64, 64), 64)
    own_high, own_low = w_high[rows, :], w_low[rows, :]
    own_ref[...] = product(own_high, own_low, high_ref[...], low_ref[...]).reshape(own_ref.shape)
    own_copy = pltpu.make_async_copy(own_ref, out.at[:, me], sems.at[0])
    own_copy.start()
    far_ref[...] = product(own_high, own_low, far_high[...], far_low[...]).reshape(far_ref.shape)
    far_copy = pltpu.make_async_copy(
        far_ref, out.at[:, lax.rem(me + 2, 4), :, pl.ds(0, NEAR)], sems.at[1]
    )
    far_copy.start()
    own_copy.wait()
    far_copy.wait()


def own_parts(me, w_high, w_low, high, low, pieces):
    columns = high.shape[-1]
    return pl.pallas_call(
        own_kernel,
        in_specs=[SMEM] + [FULL] * (4 + len(pieces)),
        out_specs=HBM,
        out_shape=jax.ShapeDtypeStruct((8, 4, 8, columns), jnp.float32),
        scratch_shapes=[
            pltpu.VMEM((8, 8, columns), jnp.float32),
            pltpu.VMEM((8, 8, NEAR), jnp.float32),
            pltpu.VMEM((8 * NV, NEAR), jnp.bfloat16),
            pltpu.VMEM((8 * NV, NEAR), jnp.bfloat16),
            pltpu.SemaphoreType.DMA((2,)),
        ],
        compiler_params=params(),
    )(me, w_high, w_low, high, low, *pieces)


def assemble_kernel(me_ref, own_ref, before_ref, across_ref, after_ref, out, sems):
    me = me_ref[0]
    width = across_ref.shape[2]
    far = out.at[:, lax.rem(me + 2, 4), :, pl.ds(out.shape[3] - width, width)]
    copies = [
        pltpu.make_async_copy(before_ref, out.at[:, lax.rem(me + 3, 4)], sems.at[0]),
        pltpu.make_async_copy(after_ref, out.at[:, lax.rem(me + 1, 4)], sems.at[1]),
        pltpu.make_async_copy(across_ref, far, sems.at[2]),
    ]
    for copy in copies:
        copy.start()
    for copy in copies:
        copy.wait()


def assemble(me, own, before, across, after):
    return pl.pallas_call(
        assemble_kernel,
        in_specs=[SMEM, HBM] + [pl.BlockSpec(memory_space=pl.ANY)] * 3,
        out_specs=HBM,
        out_shape=jax.ShapeDtypeStruct(own.shape, own.dtype),
        scratch_shapes=[pltpu.SemaphoreType.DMA((3,))],
        input_output_aliases={1: 0},
        compiler_params=params(),
    )(me, own, before, across, after)


def shifted(block, shift):
    return lax.ppermute(block, "vec", [(i, (i + shift) % 4) for i in range(4)])


def exchange(blocks):
    moved = {shift: shifted(blocks[shift], shift) for shift in (2, 1, 3)}
    return [blocks[0], moved[1], moved[2], moved[3]]


def opposite(blocks):
    one = lax.ppermute(blocks[3], "vec", [(0, 1), (1, 2), (2, 3)])
    two = lax.ppermute(blocks[0], "vec", [(0, 2), (1, 3)])
    three = lax.ppermute(blocks[1], "vec", [(0, 3)])
    return [blocks[2], one, two, three]


def all_terms(copies):
    return lax.all_to_all(copies, ("rows", "vec"), 0, 0, tiled=True)


CHUNKS = (2, 6)
NEAR = 2048


def per_device(lattice_state, constant_field, tangents):
    me = lax.axis_index("vec").astype(jnp.int32).reshape(1)
    rows, columns = lattice_state.shape[1:]
    scale = math.sqrt(2.0 * rows * lax.axis_size("rows") * columns)
    sources = (lattice_state[None], constant_field[None], tangents[: CHUNKS[0]])
    ahead = neighbours(
        *(jnp.concatenate(parts, axis=0) for parts in zip(*(edges(part) for part in sources)))
    )
    ahead, rest = lax.optimization_barrier((ahead, edges(tangents[CHUNKS[0] :])))
    halos = [ahead, neighbours(*rest)]
    pieces, local, start = [], [], 0
    for count, halo in zip(CHUNKS, halos):
        if pieces:
            halo, blocks = lax.optimization_barrier((halo, blocks))
            blocks = push(me, tangents, halo, twice, start, count)
        else:
            blocks, twice, next_state = push_first(
                me, lattice_state, constant_field, tangents, halo, count
            )
        if pieces:
            blocks, pieces = lax.optimization_barrier((blocks, pieces))
        local.append(blocks)
        pieces += exchange(blocks)
        start += count
    slabs = [
        jnp.concatenate([blocks[shift][:, :, :NEAR] for blocks in local], axis=0)
        for shift in range(4)
    ]
    slabs, pieces[5] = lax.optimization_barrier((slabs, pieces[5]))
    far = opposite(slabs)
    high, low, copies = inner_products(me, pieces, len(CHUNKS))
    terms, far = lax.optimization_barrier((all_terms(copies), far))
    growth, w_high, w_low, following, across, previous = factorise(me, terms, high, low, scale)
    across = shifted(across, 2)
    before = shifted(following, 1)
    after = shifted(previous, 3)
    own = own_parts(me, w_high, w_low, high, low, far)
    basis = assemble(me, own, before, across, after)
    return (next_state, basis.reshape(tangents.shape), growth.reshape(NV))


def solution(mesh):
    return jax.shard_map(
        per_device,
        mesh=mesh,
        in_specs=(P(None, "rows", None), P(None, "rows", None), P("vec", None, "rows", None)),
        out_specs=(P(None, "rows", None), P("vec", None, "rows", None), P()),
        check_vma=False,
    )
```
